32 devices in a mesh: parts: 2 (over y), ctx: 4 (over z), head: 2 (over x), sub: 2 (over core).
Axes of the slice: x: 2, y: 2, z: 4, core: 2. Of those that a mesh axis runs over, the one named last changes fastest.
Arguments:
- queries: bfloat16 [1024, 12288], P(('parts', 'ctx'), ('head', 'sub')), parts along dimension 0, may hold values from -250 to 250
- latent: bfloat16 [1024, 512], P(('parts', 'ctx')), parts along dimension 0, may hold values from -6 to 6
- rope_keys: bfloat16 [1024, 64], P(('parts', 'ctx')), parts along dimension 0, may hold values from -4 to 4
- latent_gain: float32 [512], replicated, may hold values from 0.1 to 1.9
- up_weight: bfloat16 [512, 16384], P(None, ('head', 'sub')), may hold values from -0.25 to 0.25
- prompt_length: int32 [2], P('parts'), parts along dimension 0, may hold values from 256 to 512
Outputs:
- attended: bfloat16 [1024, 8192], P(('parts', 'ctx'), ('head', 'sub')), parts along dimension 0
The draws below stay inside these ranges and needn't reach their ends.
There are 2 independent parts, one for each index of `parts`. The reference program is written for one: setup_inputs(seed, part) draws one part's arguments, and reference() takes and returns one part's arrays. A program takes and returns all parts, laid end to end along the dimension named above; an argument that names none is the same for every part. Nothing has to cross between parts.
All inputs are finite; a program needn't handle non-finite values.
Results may differ from the reference program's by a relative error of at most 0.012.
Values may be sent and summed in bfloat16 or wider, within the bound.
A program may use at most 128 MiB of HBM per device.

```python
import math
import jax
import jax.numpy as jnp
from jax import lax

HEADS = 64
LATENT = 512
ROPE = 64
NOPE = 128
VDIM = 128
SEQ = 512


def rope_pair(key):
    drawn_key = jax.random.fold_in(key, 11)
    drawn_rope = jnp.clip(jax.random.normal(drawn_key, (SEQ, ROPE), jnp.float32), -4.0, 4.0)
    return drawn_rope


def draw_rope_keys(key, part):
    drawn_rope = rope_pair(key)
    return drawn_rope.astype(jnp.bfloat16)


def draw_queries(key, part):
    background_key = jax.random.fold_in(key, 13)
    background = jnp.clip(2.5 * jax.random.normal(background_key, (SEQ, HEADS, NOPE + ROPE), jnp.float32), -10.0, 10.0)
    return background.reshape(SEQ, HEADS * (NOPE + ROPE)).astype(jnp.bfloat16)


def shard_levels(rng, extent, split, low, largest):
    level = 1.0
    for position, blocks in split:
        draws = jax.random.uniform(jax.random.fold_in(jax.random.fold_in(rng, 6), position), (blocks,), jnp.float32, low / len(split), largest / len(split))
        level = level * jnp.repeat(jnp.exp(draws), extent[position] // blocks).reshape((-1,) + (1,) * (len(extent) - 1 - position))
    return level


def scatter_about(rng, dims, deviation, most, split=(), kind=jnp.bfloat16):
    level = shard_levels(rng, dims, split, -0.22, 0.18) if split else 1.0
    drawn = jax.random.normal(rng, dims, jnp.float32) * deviation * level
    return jnp.minimum(jnp.maximum(drawn, -most), most).astype(kind)


def setup_inputs(seed: int = 0, part: int = 0) -> dict:
    seeds = jax.random.split(jax.random.key(seed), 7)
    own_keys = jax.random.split(jax.random.fold_in(seeds[6], part), 7)
    queries = draw_queries(jax.random.fold_in(jax.random.fold_in(seeds[6], part), 71), part)
    latent = scatter_about(own_keys[1], (SEQ, LATENT), 1.0, 6.0, ((0, 4),))
    rope_keys = draw_rope_keys(jax.random.fold_in(jax.random.fold_in(seeds[6], part), 71), part)
    latent_gain = jnp.clip(1.0 + 0.18 * jax.random.normal(seeds[3], (LATENT,), jnp.float32), 0.1, 1.9)
    up_weight = scatter_about(seeds[4], (LATENT, HEADS * (NOPE + VDIM)), LATENT ** -0.5, 0.25, ((1, 4),))
    prompt_length = jax.random.randint(own_keys[5], (1,), SEQ // 2, SEQ + 1).astype(jnp.int32)
    return dict(queries=queries, latent=latent, rope_keys=rope_keys, latent_gain=latent_gain, up_weight=up_weight, prompt_length=prompt_length)


def rotate(values, positions):
    half_width = values.shape[-1] // 2
    frequency = 10000.0 ** (-jnp.arange(half_width, dtype=jnp.float32) / half_width)
    angles = positions.astype(jnp.float32)[..., None] * frequency
    cosines = jnp.cos(angles)
    sines = jnp.sin(angles)
    lower_half = values[..., :half_width]
    upper_half = values[..., half_width:]
    return jnp.concatenate([lower_half * cosines - upper_half * sines, lower_half * sines + upper_half * cosines], -1)

def reference(queries, latent, rope_keys, latent_gain, up_weight, prompt_length):
    positions = jnp.arange(SEQ, dtype=jnp.int32)
    length = prompt_length[0]
    widened = latent.astype(jnp.float32)
    normed = (widened * lax.rsqrt(lax.optimization_barrier(jnp.mean(widened * widened, -1, keepdims=True)) + 1e-06) * latent_gain.astype(jnp.float32)).astype(jnp.bfloat16)
    key_rope = rotate(rope_keys.astype(jnp.float32), positions).astype(jnp.bfloat16)
    grouped = queries.reshape(SEQ, HEADS, NOPE + ROPE)
    query_nope = grouped[:, :, :NOPE]
    query_rope = rotate(grouped[:, :, NOPE:].astype(jnp.float32), positions[:, None]).astype(jnp.bfloat16)
    expanded = jnp.dot(normed, up_weight, preferred_element_type=jnp.float32).astype(jnp.bfloat16)
    expanded = expanded.reshape(SEQ, HEADS, NOPE + VDIM)
    allowed = (positions[None, :] <= positions[:, None]) & (positions[None, :] < length)
    scale_factor = 1.0 / math.sqrt(NOPE + ROPE)

    def one_head(head_items):
        nope_rows, rope_rows, keys_values = head_items
        scores = jnp.dot(nope_rows, keys_values[:, :NOPE].T, preferred_element_type=jnp.float32)
        scores = scores + jnp.dot(rope_rows, key_rope.T, preferred_element_type=jnp.float32)
        scores = jnp.where(allowed, scores * scale_factor, -1e+30)
        highest = lax.optimization_barrier(jnp.max(scores, -1, keepdims=True))
        raw_weights = jnp.where(allowed, jnp.exp(scores - highest), 0.0)
        running_sum = lax.optimization_barrier(jnp.sum(raw_weights, -1))
        mixed = jnp.dot(raw_weights.astype(jnp.bfloat16), keys_values[:, NOPE:], preferred_element_type=jnp.float32)
        return mixed / running_sum[:, None]
    head_outputs = lax.map(one_head, (query_nope.transpose(1, 0, 2), query_rope.transpose(1, 0, 2), expanded.transpose(1, 0, 2)))
    head_outputs = jnp.where(positions[None, :, None] < length, head_outputs, 0.0)
    return head_outputs.astype(jnp.bfloat16).transpose(1, 0, 2).reshape(SEQ, HEADS * VDIM)
```

```python
import functools
import math

import jax
import jax.numpy as jnp
from jax import lax
from jax.experimental import pallas as pl
from jax.experimental.pallas import tpu as pltpu
from jax.sharding import PartitionSpec as P

ROPE = 64
NOPE = 128
VDIM = 128
QDIM = NOPE + ROPE
KVDIM = NOPE + VDIM
MESH = pl.DeviceIdType.MESH
SCORE_SCALE = math.log2(math.e) / math.sqrt(NOPE + ROPE)


def angle_tables(first_pos, rows):
    lane8 = lax.broadcasted_iota(jnp.int32, (8, 2 * ROPE), 1)
    half = ROPE // 2
    frequency = jnp.exp((lane8 % half).astype(jnp.float32) * (-math.log(10000.0) / half))
    low = lax.broadcasted_iota(jnp.int32, (8, 2 * ROPE), 0).astype(jnp.float32) * frequency
    blocks = rows // 8
    lane = lax.broadcasted_iota(jnp.int32, (blocks, 2 * ROPE), 1)
    block_frequency = jnp.exp((lane % half).astype(jnp.float32) * (-math.log(10000.0) / half))
    base = (first_pos + 8 * lax.broadcasted_iota(jnp.int32, (blocks, 2 * ROPE), 0)).astype(jnp.float32)
    high = base * block_frequency
    cos_low, sin_low = jnp.cos(low), jnp.sin(low)
    cos_high, sin_high = jnp.cos(high), jnp.sin(high)
    cosines, sines = [], []
    for block in range(blocks):
        ch, sh = cos_high[block : block + 1], sin_high[block : block + 1]
        cosines.append(ch * cos_low - sh * sin_low)
        sines.append(sh * cos_low + ch * sin_low)
    cosine = jnp.concatenate(cosines, 0)
    sine = jnp.concatenate(sines, 0)
    lane = lax.broadcasted_iota(jnp.int32, (rows, 2 * ROPE), 1)
    return cosine, jnp.where(lane % ROPE < half, -sine, sine)


def rotate_pair(values, cosine, sine):
    half = ROPE // 2
    lane = lax.broadcasted_iota(jnp.int32, values.shape, 1)
    swapped = jnp.where(
        lane % ROPE < half, pltpu.roll(values, 2 * ROPE - half, 1), pltpu.roll(values, half, 1)
    )
    return values * cosine + swapped * sine


def kernel(
    n, n_head, n_sub, chunk,
    length_ref, queries, latent, rope_keys, latent_gain, up_weight, out,
    keys, q_raw, q_ready, w_buf, lat_buf, rope_buf, gain_buf, out_buf,
    load_sem, w_sem, out_sem, z_send, z_recv, x_send, x_recv, s_send, s_recv,
):
    ctx = lax.axis_index("ctx")
    head = lax.axis_index("head")
    sub = lax.axis_index("sub")
    rows = latent.shape[0]
    width = latent.shape[1]
    pairs = w_buf.shape[0]
    pair_w = 2 * KVDIM
    pair_q = 2 * QDIM
    piece = rows // (n_head * n_sub)

    loads = [
        pltpu.make_async_copy(latent, lat_buf, load_sem.at[0]),
        pltpu.make_async_copy(rope_keys, rope_buf, load_sem.at[1]),
        pltpu.make_async_copy(latent_gain, gain_buf, load_sem.at[2]),
        pltpu.make_async_copy(queries, q_raw, load_sem.at[3]),
    ]
    for load in loads:
        load.start()

    def w_load(pair):
        return pltpu.make_async_copy(
            up_weight.at[:, pl.ds(pl.multiple_of(pair * pair_w, pair_w), pair_w)],
            w_buf.at[pair],
            w_sem.at[pair],
        )

    for pair in range(pairs):
        w_load(pair).start()

    barrier = pltpu.get_barrier_semaphore()
    for other in range(n - 1):

        @pl.when(other < ctx)
        def _():
            pl.semaphore_signal(barrier, inc=1, device_id={"ctx": other}, device_id_type=MESH)

    @pl.when(ctx > 0)
    def _():
        for step in range(1, n_head):
            pl.semaphore_signal(
                barrier, inc=1, device_id={"head": lax.rem(head + step, n_head)}, device_id_type=MESH
            )
        for step in range(1, n_sub):
            pl.semaphore_signal(
                barrier, inc=1, device_id={"sub": lax.rem(sub + step, n_sub)}, device_id_type=MESH
            )

    cosine, sine = angle_tables(ctx * rows, rows)

    loads[0].wait()
    loads[1].wait()
    loads[2].wait()
    widened = lat_buf[...].astype(jnp.float32)
    mean = jnp.mean(widened * widened, -1, keepdims=True)
    normed = (widened * lax.rsqrt(mean + 1e-06) * gain_buf[...].reshape(1, width)).astype(jnp.bfloat16)
    rope = rope_buf[...].astype(jnp.float32)
    rotated = rotate_pair(jnp.concatenate([rope, rope], 1), cosine, sine).astype(jnp.bfloat16)
    own = pl.ds(pl.multiple_of(ctx * rows, rows), rows)
    keys[own, pl.ds(0, width)] = normed
    keys[own, pl.ds(width, 2 * ROPE)] = rotated

    waits = jnp.where(ctx > 0, n_head - 1 + n_sub - 1, 0) + (n - 1 - ctx)
    pl.semaphore_wait(barrier, waits)

    def rows_of(shard, x, s):
        return pl.ds(pl.multiple_of(shard * rows + (x * n_sub + s) * piece, piece), piece)

    def z_copy(shard, target):
        where = keys.at[rows_of(shard, head, sub)]
        return pltpu.make_async_remote_copy(
            where, where, z_send.at[target], z_recv.at[shard],
            device_id={"ctx": target}, device_id_type=MESH,
        )

    def x_copy(shard, x, step):
        where = keys.at[rows_of(shard, x, sub)]
        return pltpu.make_async_remote_copy(
            where, where, x_send.at[shard, step], x_recv.at[shard, x],
            device_id={"head": lax.rem(head + step, n_head)}, device_id_type=MESH,
        )

    def s_copy(shard, x, s, step):
        where = keys.at[rows_of(shard, x, s)]
        return pltpu.make_async_remote_copy(
            where, where, s_send.at[shard, x, step], s_recv.at[shard, x, s],
            device_id={"sub": lax.rem(sub + step, n_sub)}, device_id_type=MESH,
        )

    for target in range(n - 1, 0, -1):

        @pl.when(ctx < target)
        def _():
            z_copy(ctx, target).start()

    for shard in range(1, n):

        @pl.when(ctx < shard)
        def _():
            keys[pl.ds(shard * rows, rows), :] = jnp.zeros((rows, width + 2 * ROPE), jnp.bfloat16)

    loads[3].wait()
    lane = lax.broadcasted_iota(jnp.int32, (rows, 2 * ROPE), 1)
    lower = lane < ROPE

    def ready(pair, carry):
        at = pl.multiple_of(pair * pair_q, 128)
        tile1 = q_raw[:, pl.ds(at + NOPE, 128)].astype(jnp.float32)
        tile2 = q_raw[:, pl.ds(at + 2 * NOPE, 128)].astype(jnp.float32)
        spun = rotate_pair(jnp.where(lower, tile1, tile2), cosine, sine)
        q_ready[2 * pair, :, :NOPE] = q_raw[:, pl.ds(at, NOPE)]
        q_ready[2 * pair, :, NOPE:] = jnp.where(lower, spun, 0.0).astype(jnp.bfloat16)
        q_ready[2 * pair + 1, :, :NOPE] = pltpu.roll(
            jnp.where(lower, tile2, tile1), ROPE, 1
        ).astype(jnp.bfloat16)
        q_ready[2 * pair + 1, :, NOPE:] = jnp.where(lower, 0.0, spun).astype(jnp.bfloat16)
        return carry

    lax.fori_loop(0, pairs, ready, 0)

    for shard in range(n - 2, -1, -1):

        @pl.when(shard < ctx)
        def _():
            z_copy(shard, ctx).wait_recv()
            for step in range(1, n_head):
                x_copy(shard, head, step).start()
            for step in range(1, n_sub):
                s_copy(shard, head, sub, step).start()

    for shard in range(n - 2, -1, -1):

        @pl.when(shard < ctx)
        def _():
            for step in range(1, n_head):
                x = lax.rem(head + step, n_head)
                x_copy(shard, x, step).wait_recv()
                for s_step in range(1, n_sub):
                    s_copy(shard, x, sub, s_step).start()

    for shard in range(n - 2, -1, -1):

        @pl.when(shard < ctx)
        def _():
            for x in range(n_head):
                for s_step in range(1, n_sub):
                    s_copy(shard, x, lax.rem(sub + s_step, n_sub), s_step).wait_recv()

    length = length_ref[0]
    row_pos = ctx * rows + lax.broadcasted_iota(jnp.int32, (rows, 1), 0)
    last_key = jnp.minimum(row_pos, length - 1)
    live = row_pos < length
    n_chunks = n * rows // chunk

    def expand(pair, chunk_index):
        at = pl.multiple_of(chunk_index * chunk, chunk)
        block = pl.ds(at, chunk)
        expanded = jnp.dot(
            keys[block, pl.ds(0, width)], w_buf[pair], preferred_element_type=jnp.float32
        ).astype(jnp.bfloat16)
        allowed = at + lax.broadcasted_iota(jnp.int32, (rows, chunk), 1) <= last_key
        return expanded, keys[block, pl.ds(width, 2 * ROPE)], allowed

    def head_scores(pair, which, expanded, key_rope, allowed):
        k = jnp.concatenate([expanded[:, which * KVDIM : which * KVDIM + NOPE], key_rope], 1)
        scores = lax.dot_general(
            q_ready[2 * pair + which], k, (((1,), (1,)), ((), ())), preferred_element_type=jnp.float32
        )
        return jnp.where(allowed, scores, -1e30)

    def head_mix(which, weights, expanded):
        values = expanded[:, which * KVDIM + NOPE : (which + 1) * KVDIM]
        v = jnp.concatenate([values, jnp.ones_like(values)], 1)
        return jnp.dot(weights.astype(jnp.bfloat16), v, preferred_element_type=jnp.float32)

    def finish(pair, which, mixed):
        result = jnp.where(live, mixed[:, :VDIM] / mixed[:, VDIM:], 0.0)
        out_buf[pair, :, which * VDIM : (which + 1) * VDIM] = result.astype(jnp.bfloat16)

    def out_copy(pair):
        return pltpu.make_async_copy(
            out_buf.at[pair],
            out.at[:, pl.ds(pl.multiple_of(pair * 2 * VDIM, 2 * VDIM), 2 * VDIM)],
            out_sem.at[pair],
        )

    def attend(pair, carry):
        w_load(pair).wait()
        if n_chunks == 1:
            expanded, key_rope, allowed = expand(pair, 0)
            for which in range(2):
                scores = head_scores(pair, which, expanded, key_rope, allowed)
                top = jnp.max(scores, -1, keepdims=True)
                weights = jnp.exp2((scores - top) * SCORE_SCALE)
                finish(pair, which, head_mix(which, weights, expanded))
        else:

            def one_chunk(chunk_index, state):
                expanded, key_rope, allowed = expand(pair, chunk_index)
                later = []
                for which in range(2):
                    top, mixed = state[which]
                    scores = head_scores(pair, which, expanded, key_rope, allowed)
                    new_top = jnp.maximum(top, jnp.max(scores, -1, keepdims=True))
                    weights = jnp.exp2((scores - new_top) * SCORE_SCALE)
                    fade = jnp.exp2((top - new_top) * SCORE_SCALE)
                    later.append((new_top, mixed * fade + head_mix(which, weights, expanded)))
                return tuple(later)

            blank = (jnp.full((rows, 1), -1e30, jnp.float32), jnp.zeros((rows, 2 * VDIM), jnp.float32))
            needed = (ctx * rows) // chunk + 1
            state = lax.fori_loop(0, needed, one_chunk, (blank, blank))
            for which in range(2):
                finish(pair, which, state[which][1])
        out_copy(pair).start()
        return carry

    lax.fori_loop(0, pairs, attend, 0)

    for pair in range(pairs):
        out_copy(pair).wait()
    for target in range(n - 1, 0, -1):

        @pl.when(ctx < target)
        def _():
            z_copy(ctx, target).wait_send()

    for shard in range(n - 2, -1, -1):

        @pl.when(shard < ctx)
        def _():
            for step in range(1, n_head):
                x_copy(shard, head, step).wait_send()
            for step in range(1, n_sub):
                for x in range(n_head):
                    s_copy(shard, x, sub, step).wait_send()


def per_device(n, n_head, n_sub, queries, latent, rope_keys, latent_gain, up_weight, prompt_length):
    rows, width = latent.shape
    pairs = up_weight.shape[1] // (2 * KVDIM)
    heads = 2 * pairs
    tokens = n * rows
    chunk = tokens if tokens <= 512 else (512 if tokens % 512 == 0 else rows)
    anywhere = pl.BlockSpec(memory_space=pl.ANY)
    dma = pltpu.SemaphoreType.DMA
    cost = pl.CostEstimate(
        flops=2 * tokens * width * up_weight.shape[1] + 2 * heads * rows * tokens * (QDIM + VDIM),
        bytes_accessed=2 * (queries.size + up_weight.size + rows * heads * VDIM),
        transcendentals=heads * rows * tokens,
    )
    return pl.pallas_call(
        functools.partial(kernel, n, n_head, n_sub, chunk),
        out_shape=jax.ShapeDtypeStruct((rows, heads * VDIM), jnp.bfloat16),
        in_specs=[pl.BlockSpec(memory_space=pltpu.SMEM)] + [anywhere] * 5,
        out_specs=anywhere,
        scratch_shapes=[
            pltpu.VMEM((tokens, width + 2 * ROPE), jnp.bfloat16),
            pltpu.VMEM(queries.shape, jnp.bfloat16),
            pltpu.VMEM((heads, rows, NOPE + 2 * ROPE), jnp.bfloat16),
            pltpu.VMEM((pairs, width, 2 * KVDIM), jnp.bfloat16),
            pltpu.VMEM((rows, width), jnp.bfloat16),
            pltpu.VMEM((rows, ROPE), jnp.bfloat16),
            pltpu.VMEM((width,), jnp.float32),
            pltpu.VMEM((pairs, rows, 2 * VDIM), jnp.bfloat16),
            dma((4,)),
            dma((pairs,)),
            dma((pairs,)),
            dma((n,)),
            dma((n,)),
            dma((n, n_head)),
            dma((n, n_head)),
            dma((n, n_head, n_sub)),
            dma((n, n_head, n_sub)),
        ],
        compiler_params=pltpu.CompilerParams(
            collective_id=0, has_side_effects=True, vmem_limit_bytes=48 * 1024 * 1024
        ),
        cost_estimate=cost,
        name="mla_prefill",
    )(prompt_length, queries, latent, rope_keys, latent_gain, up_weight)


def solution(mesh):
    placed = (
        P(("parts", "ctx"), ("head", "sub")),
        P(("parts", "ctx"), None),
        P(("parts", "ctx"), None),
        P(),
        P(None, ("head", "sub")),
        P("parts"),
    )
    return jax.shard_map(
        functools.partial(per_device, mesh.shape["ctx"], mesh.shape["head"], mesh.shape["sub"]),
        mesh=mesh,
        in_specs=placed,
        out_specs=P(("parts", "ctx"), ("head", "sub")),
        check_vma=False,
    )
```

```python
import functools
import math

import jax
import jax.numpy as jnp
from jax import lax
from jax.experimental import pallas as pl
from jax.experimental.pallas import tpu as pltpu
from jax.sharding import PartitionSpec as P

ROPE = 64
NOPE = 128
VDIM = 128
QDIM = NOPE + ROPE
KVDIM = NOPE + VDIM
MESH = pl.DeviceIdType.MESH
SCORE_SCALE = math.log2(math.e) / math.sqrt(NOPE + ROPE)


def angle_tables(first_pos, rows):
    lane8 = lax.broadcasted_iota(jnp.int32, (8, 2 * ROPE), 1)
    half = ROPE // 2
    frequency = jnp.exp((lane8 % half).astype(jnp.float32) * (-math.log(10000.0) / half))
    low = lax.broadcasted_iota(jnp.int32, (8, 2 * ROPE), 0).astype(jnp.float32) * frequency
    blocks = rows // 8
    lane = lax.broadcasted_iota(jnp.int32, (blocks, 2 * ROPE), 1)
    block_frequency = jnp.exp((lane % half).astype(jnp.float32) * (-math.log(10000.0) / half))
    base = (first_pos + 8 * lax.broadcasted_iota(jnp.int32, (blocks, 2 * ROPE), 0)).astype(jnp.float32)
    high = base * block_frequency
    cos_low, sin_low = jnp.cos(low), jnp.sin(low)
    cos_high, sin_high = jnp.cos(high), jnp.sin(high)
    cosines, sines = [], []
    for block in range(blocks):
        ch, sh = cos_high[block : block + 1], sin_high[block : block + 1]
        cosines.append(ch * cos_low - sh * sin_low)
        sines.append(sh * cos_low + ch * sin_low)
    cosine = jnp.concatenate(cosines, 0)
    sine = jnp.concatenate(sines, 0)
    lane = lax.broadcasted_iota(jnp.int32, (rows, 2 * ROPE), 1)
    return cosine, jnp.where(lane % ROPE < half, -sine, sine)


def rotate_pair(values, cosine, sine):
    half = ROPE // 2
    lane = lax.broadcasted_iota(jnp.int32, values.shape, 1)
    swapped = jnp.where(
        lane % ROPE < half, pltpu.roll(values, 2 * ROPE - half, 1), pltpu.roll(values, half, 1)
    )
    return values * cosine + swapped * sine


def kernel(
    n, n_head, n_sub, chunk,
    length_ref, queries, latent, rope_keys, latent_gain, up_weight, out,
    keys, q_raw, q_ready, w_buf, kv_own, kv_even, kv_odd, lat_buf, rope_buf, gain_buf, out_buf,
    load_sem, w_sem, out_sem, z_send, z_recv, x_send, x_recv, s_send, s_recv,
):
    ctx = lax.axis_index("ctx")
    head = lax.axis_index("head")
    sub = lax.axis_index("sub")
    rows = latent.shape[0]
    width = latent.shape[1]
    pairs = w_buf.shape[0]
    pair_w = 2 * KVDIM
    pair_q = 2 * QDIM
    piece = rows // (n_head * n_sub)
    others = (n - 1) * rows
    n_chunks = n * rows // chunk

    loads = [
        pltpu.make_async_copy(latent, lat_buf, load_sem.at[0]),
        pltpu.make_async_copy(rope_keys, rope_buf, load_sem.at[1]),
        pltpu.make_async_copy(latent_gain, gain_buf, load_sem.at[2]),
        pltpu.make_async_copy(queries, q_raw, load_sem.at[3]),
    ]
    for load in loads:
        load.start()

    def w_load(pair):
        return pltpu.make_async_copy(
            up_weight.at[:, pl.ds(pl.multiple_of(pair * pair_w, pair_w), pair_w)],
            w_buf.at[pair],
            w_sem.at[pair],
        )

    for pair in range(pairs):
        w_load(pair).start()

    barrier = pltpu.get_barrier_semaphore()
    for other in range(n - 1):

        @pl.when(other < ctx)
        def _():
            pl.semaphore_signal(barrier, inc=1, device_id={"ctx": other}, device_id_type=MESH)

    @pl.when(ctx > 0)
    def _():
        for step in range(1, n_head):
            pl.semaphore_signal(
                barrier, inc=1, device_id={"head": lax.rem(head + step, n_head)}, device_id_type=MESH
            )
        for step in range(1, n_sub):
            pl.semaphore_signal(
                barrier, inc=1, device_id={"sub": lax.rem(sub + step, n_sub)}, device_id_type=MESH
            )

    cosine, sine = angle_tables(ctx * rows, rows)

    loads[0].wait()
    loads[1].wait()
    loads[2].wait()
    widened = lat_buf[...].astype(jnp.float32)
    mean = jnp.mean(widened * widened, -1, keepdims=True)
    normed = (widened * lax.rsqrt(mean + 1e-06) * gain_buf[...].reshape(1, width)).astype(jnp.bfloat16)
    rope = rope_buf[...].astype(jnp.float32)
    rope = jnp.concatenate([rope, rope], 0).T
    rotated = rotate_pair(rope, cosine, sine).astype(jnp.bfloat16)
    own = pl.ds(others, rows)
    keys[own, pl.ds(0, width)] = normed
    keys[own, pl.ds(width, 2 * ROPE)] = rotated

    waits = jnp.where(ctx > 0, n_head - 1 + n_sub - 1, 0) + (n - 1 - ctx)
    pl.semaphore_wait(barrier, waits)

    def rows_of(slot, x, s):
        return pl.ds(pl.multiple_of(slot * rows + (x * n_sub + s) * piece, piece), piece)

    def z_copy(shard, target):
        return pltpu.make_async_remote_copy(
            keys.at[rows_of(n - 1, head, sub)], keys.at[rows_of(shard, head, sub)],
            z_send.at[target], z_recv.at[shard],
            device_id={"ctx": target}, device_id_type=MESH,
        )

    def x_copy(shard, x, step):
        where = keys.at[rows_of(shard, x, sub)]
        return pltpu.make_async_remote_copy(
            where, where, x_send.at[shard, step], x_recv.at[shard, x],
            device_id={"head": lax.rem(head + step, n_head)}, device_id_type=MESH,
        )

    def s_copy(shard, x, s, step):
        where = keys.at[rows_of(shard, x, s)]
        return pltpu.make_async_remote_copy(
            where, where, s_send.at[shard, x, step], s_recv.at[shard, x, s],
            device_id={"sub": lax.rem(sub + step, n_sub)}, device_id_type=MESH,
        )

    for target in range(n - 1, 0, -1):

        @pl.when(ctx < target)
        def _():
            z_copy(ctx, target).start()

    for slot in range(n - 1):

        @pl.when(ctx <= slot)
        def _():
            keys[pl.ds(slot * rows, rows), :] = jnp.zeros((rows, width + 2 * ROPE), jnp.bfloat16)

    loads[3].wait()
    lane = lax.broadcasted_iota(jnp.int32, (rows, 2 * ROPE), 1)
    lower = lane < ROPE

    def ready(pair, carry):
        at = pl.multiple_of(pair * pair_q, 128)
        tile1 = q_raw[:, pl.ds(at + NOPE, 128)].astype(jnp.float32)
        tile2 = q_raw[:, pl.ds(at + 2 * NOPE, 128)].astype(jnp.float32)
        spun = rotate_pair(jnp.where(lower, tile1, tile2), cosine, sine)
        q_ready[2 * pair, :, :NOPE] = q_raw[:, pl.ds(at, NOPE)]
        q_ready[2 * pair, :, NOPE:] = jnp.where(lower, spun, 0.0).astype(jnp.bfloat16)
        q_ready[2 * pair + 1, :, :NOPE] = pltpu.roll(
            jnp.where(lower, tile2, tile1), ROPE, 1
        ).astype(jnp.bfloat16)
        q_ready[2 * pair + 1, :, NOPE:] = jnp.where(lower, 0.0, spun).astype(jnp.bfloat16)
        return carry

    lax.fori_loop(0, pairs, ready, 0)

    def project(block, pair):
        return jnp.dot(
            keys[block, pl.ds(0, width)], w_buf[pair], preferred_element_type=jnp.float32
        ).astype(jnp.bfloat16)

    def expand_own(pair, carry):
        w_load(pair).wait()
        kv_own[pair] = project(own, pair)
        return carry

    half = pairs // 2
    lax.fori_loop(0, half, expand_own, 0)

    for shard in range(n - 2, -1, -1):

        @pl.when(shard < ctx)
        def _():
            z_copy(shard, ctx).wait_recv()
            for step in range(1, n_head):
                x_copy(shard, head, step).start()
            for step in range(1, n_sub):
                s_copy(shard, head, sub, step).start()

    lax.fori_loop(half, pairs, expand_own, 0)

    for shard in range(n - 2, -1, -1):

        @pl.when(shard < ctx)
        def _():
            for step in range(1, n_head):
                x = lax.rem(head + step, n_head)
                x_copy(shard, x, step).wait_recv()
                for s_step in range(1, n_sub):
                    s_copy(shard, x, sub, s_step).start()

    for shard in range(n - 2, -1, -1):

        @pl.when(shard < ctx)
        def _():
            for x in range(n_head):
                for s_step in range(1, n_sub):
                    s_copy(shard, x, lax.rem(sub + s_step, n_sub), s_step).wait_recv()

    length = length_ref[0]
    row_pos = ctx * rows + lax.broadcasted_iota(jnp.int32, (rows, 1), 0)
    last_key = jnp.minimum(row_pos, length - 1)
    live = row_pos < length

    def allowed_keys(first):
        slot_pos = first + lax.broadcasted_iota(jnp.int32, (1, chunk), 1)
        far = n * rows
        position = jnp.where(
            slot_pos >= others, slot_pos - others + ctx * rows, jnp.where(slot_pos < ctx * rows, slot_pos, far)
        )
        return position <= last_key

    def head_scores(pair, which, key_nope, key_rope, allowed):
        k = jnp.concatenate([key_nope, key_rope], 1)
        scores = lax.dot_general(
            q_ready[2 * pair + which], k, (((1,), (1,)), ((), ())), preferred_element_type=jnp.float32
        )
        return jnp.where(allowed, scores, -1e30)

    def head_mix(weights, values):
        v = jnp.concatenate([values, jnp.ones_like(values)], 1)
        return jnp.dot(weights.astype(jnp.bfloat16), v, preferred_element_type=jnp.float32)

    def finish(pair, which, mixed):
        result = jnp.where(live, mixed[:, :VDIM] / mixed[:, VDIM:], 0.0)
        out_buf[pair, :, which * VDIM : (which + 1) * VDIM] = result.astype(jnp.bfloat16)

    def out_copy(pair):
        return pltpu.make_async_copy(
            out_buf.at[pair],
            out.at[:, pl.ds(pl.multiple_of(pair * 2 * VDIM, 2 * VDIM), 2 * VDIM)],
            out_sem.at[pair],
        )

    if n_chunks == 1:
        allowed = allowed_keys(0)
        earlier = pl.ds(0, others)

        def expand(pair, kv):
            kv[earlier, :] = project(earlier, pair)
            kv[own, :] = kv_own[pair]

        def attend(pair, kv):
            scores = [
                head_scores(
                    pair, which, kv[:, which * KVDIM : which * KVDIM + NOPE], keys[:, width:], allowed
                )
                for which in range(2)
            ]
            for which in range(2):
                top = jnp.max(scores[which], -1, keepdims=True)
                weights = jnp.exp2((scores[which] - top) * SCORE_SCALE)
                mixed = head_mix(weights, kv[:, which * KVDIM + NOPE : (which + 1) * KVDIM])
                finish(pair, which, mixed)
            out_copy(pair).start()

        expand(0, kv_even)

        def two_pairs(step, carry):
            expand(2 * step + 1, kv_odd)
            attend(2 * step, kv_even)
            expand(lax.rem(2 * step + 2, pairs), kv_even)
            attend(2 * step + 1, kv_odd)
            return carry

        lax.fori_loop(0, pairs // 2, two_pairs, 0)
    else:

        def attend(pair, carry):
            needed = jnp.minimum((ctx * rows + chunk - 1) // chunk, n_chunks - 1)

            def one_chunk(step, state):
                index = jnp.where(step == needed, n_chunks - 1, step)
                at = pl.multiple_of(index * chunk, chunk)
                block = pl.ds(at, chunk)
                expanded = project(block, pair)
                allowed = allowed_keys(at)
                later = []
                for which in range(2):
                    top, mixed = state[which]
                    first = which * KVDIM
                    scores = head_scores(
                        pair, which, expanded[:, first : first + NOPE],
                        keys[block, pl.ds(width, 2 * ROPE)], allowed,
                    )
                    new_top = jnp.maximum(top, jnp.max(scores, -1, keepdims=True))
                    weights = jnp.where(allowed, jnp.exp2((scores - new_top) * SCORE_SCALE), 0.0)
                    fade = jnp.exp2((top - new_top) * SCORE_SCALE)
                    mix = head_mix(weights, expanded[:, first + NOPE : first + KVDIM])
                    later.append((new_top, mixed * fade + mix))
                return tuple(later)

            blank = (jnp.full((rows, 1), -1e30, jnp.float32), jnp.zeros((rows, 2 * VDIM), jnp.float32))
            state = lax.fori_loop(0, needed + 1, one_chunk, (blank, blank))
            for which in range(2):
                finish(pair, which, state[which][1])
            out_copy(pair).start()
            return carry

        lax.fori_loop(0, pairs, attend, 0)

    for pair in range(pairs):
        out_copy(pair).wait()
    for target in range(n - 1, 0, -1):

        @pl.when(ctx < target)
        def _():
            z_copy(ctx, target).wait_send()

    for shard in range(n - 2, -1, -1):

        @pl.when(shard < ctx)
        def _():
            for step in range(1, n_head):
                x_copy(shard, head, step).wait_send()
            for step in range(1, n_sub):
                for x in range(n_head):
                    s_copy(shard, x, sub, step).wait_send()


def per_device(n, n_head, n_sub, queries, latent, rope_keys, latent_gain, up_weight, prompt_length):
    rows, width = latent.shape
    pairs = up_weight.shape[1] // (2 * KVDIM)
    heads = 2 * pairs
    tokens = n * rows
    chunk = tokens if tokens <= 512 else (512 if tokens % 512 == 0 else rows)
    anywhere = pl.BlockSpec(memory_space=pl.ANY)
    dma = pltpu.SemaphoreType.DMA
    cost = pl.CostEstimate(
        flops=2 * tokens * width * up_weight.shape[1] + 2 * heads * rows * tokens * (QDIM + VDIM),
        bytes_accessed=2 * (queries.size + up_weight.size + rows * heads * VDIM),
        transcendentals=heads * rows * tokens,
    )
    return pl.pallas_call(
        functools.partial(kernel, n, n_head, n_sub, chunk),
        out_shape=jax.ShapeDtypeStruct((rows, heads * VDIM), jnp.bfloat16),
        in_specs=[pl.BlockSpec(memory_space=pltpu.SMEM)] + [anywhere] * 5,
        out_specs=anywhere,
        scratch_shapes=[
            pltpu.VMEM((tokens, width + 2 * ROPE), jnp.bfloat16),
            pltpu.VMEM(queries.shape, jnp.bfloat16),
            pltpu.VMEM((heads, rows, NOPE + 2 * ROPE), jnp.bfloat16),
            pltpu.VMEM((pairs, width, 2 * KVDIM), jnp.bfloat16),
            pltpu.VMEM((pairs, rows, 2 * KVDIM), jnp.bfloat16),
            pltpu.VMEM((chunk, 2 * KVDIM), jnp.bfloat16),
            pltpu.VMEM((chunk, 2 * KVDIM), jnp.bfloat16),
            pltpu.VMEM((rows, width), jnp.bfloat16),
            pltpu.VMEM((ROPE, rows), jnp.bfloat16),
            pltpu.VMEM((width,), jnp.float32),
            pltpu.VMEM((pairs, rows, 2 * VDIM), jnp.bfloat16),
            dma((4,)),
            dma((pairs,)),
            dma((pairs,)),
            dma((n,)),
            dma((n,)),
            dma((n, n_head)),
            dma((n, n_head)),
            dma((n, n_head, n_sub)),
            dma((n, n_head, n_sub)),
        ],
        compiler_params=pltpu.CompilerParams(
            collective_id=0, has_side_effects=True, vmem_limit_bytes=63 * 1024 * 1024
        ),
        cost_estimate=cost,
        name="mla_prefill",
    )(prompt_length, queries, latent, rope_keys.T, latent_gain, up_weight)


def solution(mesh):
    placed = (
        P(("parts", "ctx"), ("head", "sub")),
        P(("parts", "ctx"), None),
        P(("parts", "ctx"), None),
        P(),
        P(None, ("head", "sub")),
        P("parts"),
    )
    return jax.shard_map(
        functools.partial(per_device, mesh.shape["ctx"], mesh.shape["head"], mesh.shape["sub"]),
        mesh=mesh,
        in_specs=placed,
        out_specs=P(("parts", "ctx"), ("head", "sub")),
        check_vma=False,
    )
```

```python
import functools
import math

import jax
import jax.numpy as jnp
from jax import lax
from jax.experimental import pallas as pl
from jax.experimental.pallas import tpu as pltpu
from jax.sharding import PartitionSpec as P

ROPE = 64
NOPE = 128
VDIM = 128
QDIM = NOPE + ROPE
KVDIM = NOPE + VDIM
MESH = pl.DeviceIdType.MESH
SCORE_SCALE = math.log2(math.e) / math.sqrt(NOPE + ROPE)


def angle_tables(first_pos, rows):
    lane8 = lax.broadcasted_iota(jnp.int32, (8, 2 * ROPE), 1)
    half = ROPE // 2
    frequency = jnp.exp((lane8 % half).astype(jnp.float32) * (-math.log(10000.0) / half))
    low = lax.broadcasted_iota(jnp.int32, (8, 2 * ROPE), 0).astype(jnp.float32) * frequency
    blocks = rows // 8
    lane = lax.broadcasted_iota(jnp.int32, (blocks, 2 * ROPE), 1)
    block_frequency = jnp.exp((lane % half).astype(jnp.float32) * (-math.log(10000.0) / half))
    base = (first_pos + 8 * lax.broadcasted_iota(jnp.int32, (blocks, 2 * ROPE), 0)).astype(jnp.float32)
    high = base * block_frequency
    cos_low, sin_low = jnp.cos(low), jnp.sin(low)
    cos_high, sin_high = jnp.cos(high), jnp.sin(high)
    cosines, sines = [], []
    for block in range(blocks):
        ch, sh = cos_high[block : block + 1], sin_high[block : block + 1]
        cosines.append(ch * cos_low - sh * sin_low)
        sines.append(sh * cos_low + ch * sin_low)
    cosine = jnp.concatenate(cosines, 0)
    sine = jnp.concatenate(sines, 0)
    lane = lax.broadcasted_iota(jnp.int32, (rows, 2 * ROPE), 1)
    return cosine, jnp.where(lane % ROPE < half, -sine, sine)


def rotate_pair(values, cosine, sine):
    half = ROPE // 2
    lane = lax.broadcasted_iota(jnp.int32, values.shape, 1)
    swapped = jnp.where(
        lane % ROPE < half, pltpu.roll(values, 2 * ROPE - half, 1), pltpu.roll(values, half, 1)
    )
    return values * cosine + swapped * sine


def kernel(
    n, n_head, n_sub, chunk,
    length_ref, queries, latent, rope_keys, latent_gain, up_weight, out,
    keys, q_raw, q_ready, w_buf, kv, lat_buf, rope_buf, gain_buf,
    load_sem, w_sem, z_send, z_recv, x_send, x_recv, s_send, s_recv,
):
    ctx = lax.axis_index("ctx")
    head = lax.axis_index("head")
    sub = lax.axis_index("sub")
    rows = latent.shape[0]
    width = latent.shape[1]
    pairs = w_buf.shape[0]
    pair_w = 2 * KVDIM
    pair_q = 2 * QDIM
    piece = rows // (n_head * n_sub)
    others = (n - 1) * rows
    n_chunks = n * rows // chunk

    loads = [
        pltpu.make_async_copy(latent, lat_buf, load_sem.at[0]),
        pltpu.make_async_copy(rope_keys, rope_buf, load_sem.at[1]),
        pltpu.make_async_copy(latent_gain, gain_buf, load_sem.at[2]),
        pltpu.make_async_copy(queries, q_raw, load_sem.at[3]),
    ]
    for load in loads:
        load.start()

    def w_load(pair):
        return pltpu.make_async_copy(
            up_weight.at[:, pl.ds(pl.multiple_of(pair * pair_w, pair_w), pair_w)],
            w_buf.at[pair],
            w_sem.at[pair],
        )

    for pair in range(pairs):
        w_load(pair).start()

    barrier = pltpu.get_barrier_semaphore()
    for other in range(n - 1):

        @pl.when(other < ctx)
        def _():
            pl.semaphore_signal(barrier, inc=1, device_id={"ctx": other}, device_id_type=MESH)

    @pl.when(ctx > 0)
    def _():
        for step in range(1, n_head):
            pl.semaphore_signal(
                barrier, inc=1, device_id={"head": lax.rem(head + step, n_head)}, device_id_type=MESH
            )
        for step in range(1, n_sub):
            pl.semaphore_signal(
                barrier, inc=1, device_id={"sub": lax.rem(sub + step, n_sub)}, device_id_type=MESH
            )

    cosine, sine = angle_tables(ctx * rows, rows)

    loads[0].wait()
    loads[1].wait()
    loads[2].wait()
    widened = lat_buf[...].astype(jnp.float32)
    mean = jnp.mean(widened * widened, -1, keepdims=True)
    normed = (widened * lax.rsqrt(mean + 1e-06) * gain_buf[...].reshape(1, width)).astype(jnp.bfloat16)
    rope = rope_buf[...].astype(jnp.float32)
    rope = jnp.concatenate([rope, rope], 0).T
    rotated = rotate_pair(rope, cosine, sine).astype(jnp.bfloat16)
    own = pl.ds(others, rows)
    keys[own, pl.ds(0, width)] = normed
    keys[own, pl.ds(width, 2 * ROPE)] = rotated

    for slot in range(n - 1):

        @pl.when(ctx <= slot)
        def _():
            keys[pl.ds(slot * rows, rows), :] = jnp.zeros((rows, width + 2 * ROPE), jnp.bfloat16)
            if n_chunks == 1:
                kv[:, pl.ds(slot * rows, rows), :] = jnp.zeros((pairs, rows, pair_w), jnp.bfloat16)

    loads[3].wait()
    lane = lax.broadcasted_iota(jnp.int32, (rows, 2 * ROPE), 1)
    lower = lane < ROPE

    def ready(pair, carry):
        at = pl.multiple_of(pair * pair_q, 128)
        tile1 = q_raw[:, pl.ds(at + NOPE, 128)].astype(jnp.float32)
        tile2 = q_raw[:, pl.ds(at + 2 * NOPE, 128)].astype(jnp.float32)
        spun = rotate_pair(jnp.where(lower, tile1, tile2), cosine, sine)
        q_ready[2 * pair, :, :NOPE] = q_raw[:, pl.ds(at, NOPE)]
        q_ready[2 * pair, :, NOPE:] = jnp.where(lower, spun, 0.0).astype(jnp.bfloat16)
        q_ready[2 * pair + 1, :, :NOPE] = pltpu.roll(
            jnp.where(lower, tile2, tile1), ROPE, 1
        ).astype(jnp.bfloat16)
        q_ready[2 * pair + 1, :, NOPE:] = jnp.where(lower, 0.0, spun).astype(jnp.bfloat16)
        return carry

    lax.fori_loop(0, pairs, ready, 0)

    waits = jnp.where(ctx > 0, n_head - 1 + n_sub - 1, 0) + (n - 1 - ctx)
    pl.semaphore_wait(barrier, waits)

    def rows_of(slot, x, s):
        return pl.ds(pl.multiple_of(slot * rows + (x * n_sub + s) * piece, piece), piece)

    def z_copy(shard, target):
        return pltpu.make_async_remote_copy(
            keys.at[rows_of(n - 1, head, sub)], keys.at[rows_of(shard, head, sub)],
            z_send.at[target], z_recv.at[shard],
            device_id={"ctx": target}, device_id_type=MESH,
        )

    def x_copy(shard, x, step):
        where = keys.at[rows_of(shard, x, sub)]
        return pltpu.make_async_remote_copy(
            where, where, x_send.at[shard, step], x_recv.at[shard, x],
            device_id={"head": lax.rem(head + step, n_head)}, device_id_type=MESH,
        )

    def s_copy(shard, x, s, step):
        where = keys.at[rows_of(shard, x, s)]
        return pltpu.make_async_remote_copy(
            where, where, s_send.at[shard, x, step], s_recv.at[shard, x, s],
            device_id={"sub": lax.rem(sub + step, n_sub)}, device_id_type=MESH,
        )

    for target in range(n - 1, 0, -1):

        @pl.when(ctx < target)
        def _():
            z_copy(ctx, target).start()

    def project(block, pair):
        return jnp.dot(
            keys[block, pl.ds(0, width)], w_buf[pair], preferred_element_type=jnp.float32
        ).astype(jnp.bfloat16)

    def expand(slot, first, last, fresh=False):
        block = pl.ds(slot * rows, rows)

        def one(pair, carry):
            if fresh:
                w_load(pair).wait()
            kv[pair, block, :] = project(block, pair)
            return carry

        lax.fori_loop(first, last, one, 0, unroll=2)

    def pass_on(shard):
        @pl.when(shard < ctx)
        def _():
            z_copy(shard, ctx).wait_recv()
            for step in range(1, n_head):
                x_copy(shard, head, step).start()
            for step in range(1, n_sub):
                s_copy(shard, head, sub, step).start()

    def pass_to_sibling(shard):
        @pl.when(shard < ctx)
        def _():
            for step in range(1, n_head):
                x = lax.rem(head + step, n_head)
                x_copy(shard, x, step).wait_recv()
                for s_step in range(1, n_sub):
                    s_copy(shard, x, sub, s_step).start()

    def complete(shard):
        for x in range(n_head):
            for s_step in range(1, n_sub):
                s_copy(shard, x, lax.rem(sub + s_step, n_sub), s_step).wait_recv()

    order = list(range(n - 2, -1, -1))
    if n_chunks == 1:
        half = pairs // 2
        expand(n - 1, 0, half, fresh=True)
        pass_on(order[0])
        expand(n - 1, half, pairs, fresh=True)
        for earlier, later in zip(order[:-1], order[1:]):
            pass_on(later)
            pass_to_sibling(earlier)
        for place, shard in enumerate(order):
            if place == 0:

                @pl.when(shard < ctx)
                def _():
                    if len(order) > 1:
                        complete(shard)
                        expand(shard, 0, half)

                pass_to_sibling(order[-1])

                @pl.when(shard < ctx)
                def _():
                    if len(order) > 1:
                        expand(shard, half, pairs)
                    else:
                        complete(shard)
                        expand(shard, 0, pairs)

            else:

                @pl.when(shard < ctx)
                def _():
                    complete(shard)
                    expand(shard, 0, pairs)

    else:
        for pair in range(pairs):
            w_load(pair).wait()
        for shard in order:
            pass_on(shard)
        for shard in order:
            pass_to_sibling(shard)
        for shard in order:

            @pl.when(shard < ctx)
            def _():
                complete(shard)

    length = length_ref[0]
    row_pos = ctx * rows + lax.broadcasted_iota(jnp.int32, (rows, 1), 0)
    last_key = jnp.minimum(row_pos, length - 1)
    live = row_pos < length

    def allowed_keys(first):
        slot_pos = first + lax.broadcasted_iota(jnp.int32, (1, chunk), 1)
        far = n * rows
        position = jnp.where(
            slot_pos >= others, slot_pos - others + ctx * rows, jnp.where(slot_pos < ctx * rows, slot_pos, far)
        )
        return position <= last_key

    def head_scores(pair, which, key_nope, key_rope, allowed):
        k = jnp.concatenate([key_nope, key_rope], 1)
        scores = lax.dot_general(
            q_ready[2 * pair + which], k, (((1,), (1,)), ((), ())), preferred_element_type=jnp.float32
        )
        return jnp.where(allowed, scores, -1e30)

    def head_mix(weights, values):
        v = jnp.concatenate([values, jnp.ones_like(values)], 1)
        return jnp.dot(weights.astype(jnp.bfloat16), v, preferred_element_type=jnp.float32)

    def finish(pair, which, mixed):
        result = jnp.where(live, mixed[:, :VDIM] / mixed[:, VDIM:], 0.0)
        at = pl.multiple_of((2 * pair + which) * VDIM, VDIM)
        out[:, pl.ds(at, VDIM)] = result.astype(jnp.bfloat16)

    if n_chunks == 1:
        allowed = allowed_keys(0)

        def attend(pair, carry):
            scores = [
                head_scores(
                    pair, which, kv[pair, :, which * KVDIM : which * KVDIM + NOPE], keys[:, width:], allowed
                )
                for which in range(2)
            ]
            for which in range(2):
                top = jnp.max(scores[which], -1, keepdims=True)
                weights = jnp.exp2((scores[which] - top) * SCORE_SCALE)
                mixed = head_mix(weights, kv[pair, :, which * KVDIM + NOPE : (which + 1) * KVDIM])
                finish(pair, which, mixed)
            return carry

        lax.fori_loop(0, pairs, attend, 0, unroll=2)
    else:

        def attend(pair, carry):
            needed = jnp.minimum((ctx * rows + chunk - 1) // chunk, n_chunks - 1)

            def one_chunk(step, state):
                index = jnp.where(step == needed, n_chunks - 1, step)
                at = pl.multiple_of(index * chunk, chunk)
                block = pl.ds(at, chunk)
                expanded = project(block, pair)
                allowed = allowed_keys(at)
                later = []
                for which in range(2):
                    top, mixed = state[which]
                    first = which * KVDIM
                    scores = head_scores(
                        pair, which, expanded[:, first : first + NOPE],
                        keys[block, pl.ds(width, 2 * ROPE)], allowed,
                    )
                    new_top = jnp.maximum(top, jnp.max(scores, -1, keepdims=True))
                    weights = jnp.where(allowed, jnp.exp2((scores - new_top) * SCORE_SCALE), 0.0)
                    fade = jnp.exp2((top - new_top) * SCORE_SCALE)
                    mix = head_mix(weights, expanded[:, first + NOPE : first + KVDIM])
                    later.append((new_top, mixed * fade + mix))
                return tuple(later)

            blank = (jnp.full((rows, 1), -1e30, jnp.float32), jnp.zeros((rows, 2 * VDIM), jnp.float32))
            state = lax.fori_loop(0, needed + 1, one_chunk, (blank, blank))
            for which in range(2):
                finish(pair, which, state[which][1])
            return carry

        lax.fori_loop(0, pairs, attend, 0)

    for target in range(n - 1, 0, -1):

        @pl.when(ctx < target)
        def _():
            z_copy(ctx, target).wait_send()

    for shard in range(n - 2, -1, -1):

        @pl.when(shard < ctx)
        def _():
            for step in range(1, n_head):
                x_copy(shard, head, step).wait_send()
            for step in range(1, n_sub):
                for x in range(n_head):
                    s_copy(shard, x, sub, step).wait_send()


def per_device(n, n_head, n_sub, queries, latent, rope_keys, latent_gain, up_weight, prompt_length):
    rows, width = latent.shape
    pairs = up_weight.shape[1] // (2 * KVDIM)
    heads = 2 * pairs
    tokens = n * rows
    chunk = tokens if tokens <= 512 else (512 if tokens % 512 == 0 else rows)
    anywhere = pl.BlockSpec(memory_space=pl.ANY)
    dma = pltpu.SemaphoreType.DMA
    cost = pl.CostEstimate(
        flops=2 * tokens * width * up_weight.shape[1] + 2 * heads * rows * tokens * (QDIM + VDIM),
        bytes_accessed=2 * (queries.size + up_weight.size + rows * heads * VDIM),
        transcendentals=heads * rows * tokens,
    )
    return pl.pallas_call(
        functools.partial(kernel, n, n_head, n_sub, chunk),
        out_shape=pltpu.VMEM((rows, heads * VDIM), jnp.bfloat16),
        in_specs=[pl.BlockSpec(memory_space=pltpu.SMEM)] + [anywhere] * 5,
        out_specs=pl.BlockSpec(memory_space=pltpu.VMEM),
        scratch_shapes=[
            pltpu.VMEM((tokens, width + 2 * ROPE), jnp.bfloat16),
            pltpu.VMEM(queries.shape, jnp.bfloat16),
            pltpu.VMEM((heads, rows, NOPE + 2 * ROPE), jnp.bfloat16),
            pltpu.VMEM((pairs, width, 2 * KVDIM), jnp.bfloat16),
            pltpu.VMEM((pairs if chunk == tokens else 1, chunk, 2 * KVDIM), jnp.bfloat16),
            pltpu.VMEM((rows, width), jnp.bfloat16),
            pltpu.VMEM((ROPE, rows), jnp.bfloat16),
            pltpu.VMEM((width,), jnp.float32),
            dma((4,)),
            dma((pairs,)),
            dma((n,)),
            dma((n,)),
            dma((n, n_head)),
            dma((n, n_head)),
            dma((n, n_head, n_sub)),
            dma((n, n_head, n_sub)),
        ],
        compiler_params=pltpu.CompilerParams(
            collective_id=0, has_side_effects=True, vmem_limit_bytes=63 * 1024 * 1024
        ),
        cost_estimate=cost,
        name="mla_prefill",
    )(prompt_length, queries, latent, rope_keys.T, latent_gain, up_weight)


def solution(mesh):
    placed = (
        P(("parts", "ctx"), ("head", "sub")),
        P(("parts", "ctx"), None),
        P(("parts", "ctx"), None),
        P(),
        P(None, ("head", "sub")),
        P("parts"),
    )
    return jax.shard_map(
        functools.partial(per_device, mesh.shape["ctx"], mesh.shape["head"], mesh.shape["sub"]),
        mesh=mesh,
        in_specs=placed,
        out_specs=P(("parts", "ctx"), ("head", "sub")),
        check_vma=False,
    )
```

```python
import functools
import math

import jax
import jax.numpy as jnp
from jax import lax
from jax.experimental import pallas as pl
from jax.experimental.pallas import tpu as pltpu
from jax.sharding import PartitionSpec as P

ROPE = 64
NOPE = 128
VDIM = 128
QDIM = NOPE + ROPE
KVDIM = NOPE + VDIM
ONES = 16
MESH = pl.DeviceIdType.MESH
SCORE_SCALE = math.log2(math.e) / math.sqrt(NOPE + ROPE)


def angle_tables(first_pos, rows):
    lane8 = lax.broadcasted_iota(jnp.int32, (8, 2 * ROPE), 1)
    half = ROPE // 2
    frequency = jnp.exp((lane8 % half).astype(jnp.float32) * (-math.log(10000.0) / half))
    low = lax.broadcasted_iota(jnp.int32, (8, 2 * ROPE), 0).astype(jnp.float32) * frequency
    blocks = rows // 8
    lane = lax.broadcasted_iota(jnp.int32, (blocks, 2 * ROPE), 1)
    block_frequency = jnp.exp((lane % half).astype(jnp.float32) * (-math.log(10000.0) / half))
    base = (first_pos + 8 * lax.broadcasted_iota(jnp.int32, (blocks, 2 * ROPE), 0)).astype(jnp.float32)
    high = base * block_frequency
    cos_low, sin_low = jnp.cos(low), jnp.sin(low)
    cos_high, sin_high = jnp.cos(high), jnp.sin(high)
    cosines, sines = [], []
    for block in range(blocks):
        ch, sh = cos_high[block : block + 1], sin_high[block : block + 1]
        cosines.append(ch * cos_low - sh * sin_low)
        sines.append(sh * cos_low + ch * sin_low)
    cosine = jnp.concatenate(cosines, 0)
    sine = jnp.concatenate(sines, 0)
    lane = lax.broadcasted_iota(jnp.int32, (rows, 2 * ROPE), 1)
    return cosine, jnp.where(lane % ROPE < half, -sine, sine)


def rotate_pair(values, cosine, sine):
    half = ROPE // 2
    lane = lax.broadcasted_iota(jnp.int32, values.shape, 1)
    swapped = jnp.where(
        lane % ROPE < half, pltpu.roll(values, 2 * ROPE - half, 1), pltpu.roll(values, half, 1)
    )
    return values * cosine + swapped * sine


def kernel(
    n, n_head, n_sub, chunk,
    length_ref, queries, latent, rope_keys, latent_gain, up_weight, out,
    keys, q_raw, q_ready, w_buf, value_w, values_t, lat_buf, rope_buf, gain_buf,
    load_sem, w_sem, z_send, z_recv, x_send, x_recv, s_send, s_recv,
):
    ctx = lax.axis_index("ctx")
    head = lax.axis_index("head")
    sub = lax.axis_index("sub")
    rows = latent.shape[0]
    width = latent.shape[1]
    pairs = w_buf.shape[0]
    pair_w = 2 * KVDIM
    pair_q = 2 * QDIM
    piece = rows // (n_head * n_sub)
    others = (n - 1) * rows
    n_chunks = n * rows // chunk

    loads = [
        pltpu.make_async_copy(latent, lat_buf, load_sem.at[0]),
        pltpu.make_async_copy(rope_keys, rope_buf, load_sem.at[1]),
        pltpu.make_async_copy(latent_gain, gain_buf, load_sem.at[2]),
        pltpu.make_async_copy(queries, q_raw, load_sem.at[3]),
    ]
    for load in loads:
        load.start()

    def w_load(pair):
        return pltpu.make_async_copy(
            up_weight.at[:, pl.ds(pl.multiple_of(pair * pair_w, pair_w), pair_w)],
            w_buf.at[pair],
            w_sem.at[pair],
        )

    for pair in range(pairs):
        w_load(pair).start()

    barrier = pltpu.get_barrier_semaphore()
    for other in range(n - 1):

        @pl.when(other < ctx)
        def _():
            pl.semaphore_signal(barrier, inc=1, device_id={"ctx": other}, device_id_type=MESH)

    @pl.when(ctx > 0)
    def _():
        for step in range(1, n_head):
            pl.semaphore_signal(
                barrier, inc=1, device_id={"head": lax.rem(head + step, n_head)}, device_id_type=MESH
            )
        for step in range(1, n_sub):
            pl.semaphore_signal(
                barrier, inc=1, device_id={"sub": lax.rem(sub + step, n_sub)}, device_id_type=MESH
            )

    cosine, sine = angle_tables(ctx * rows, rows)

    loads[0].wait()
    loads[1].wait()
    loads[2].wait()
    widened = lat_buf[...].astype(jnp.float32)
    mean = jnp.mean(widened * widened, -1, keepdims=True)
    normed = (widened * lax.rsqrt(mean + 1e-06) * gain_buf[...].reshape(1, width)).astype(jnp.bfloat16)
    rope = rope_buf[...].astype(jnp.float32)
    rope = jnp.concatenate([rope, rope], 0).T
    rotated = rotate_pair(rope, cosine, sine).astype(jnp.bfloat16)
    own = pl.ds(others, rows)
    keys[own, pl.ds(0, width)] = normed
    keys[own, pl.ds(width, 2 * ROPE)] = rotated

    for slot in range(n - 1):

        @pl.when(ctx <= slot)
        def _():
            keys[pl.ds(slot * rows, rows), :] = jnp.zeros((rows, width + 2 * ROPE), jnp.bfloat16)

    loads[3].wait()
    lane = lax.broadcasted_iota(jnp.int32, (rows, 2 * ROPE), 1)
    lower = lane < ROPE

    def ready(pair, carry):
        at = pl.multiple_of(pair * pair_q, 128)
        tile1 = q_raw[:, pl.ds(at + NOPE, 128)].astype(jnp.float32)
        tile2 = q_raw[:, pl.ds(at + 2 * NOPE, 128)].astype(jnp.float32)
        spun = rotate_pair(jnp.where(lower, tile1, tile2), cosine, sine)
        q_ready[2 * pair, :, :NOPE] = q_raw[:, pl.ds(at, NOPE)]
        q_ready[2 * pair, :, NOPE:] = jnp.where(lower, spun, 0.0).astype(jnp.bfloat16)
        q_ready[2 * pair + 1, :, :NOPE] = pltpu.roll(
            jnp.where(lower, tile2, tile1), ROPE, 1
        ).astype(jnp.bfloat16)
        q_ready[2 * pair + 1, :, NOPE:] = jnp.where(lower, 0.0, spun).astype(jnp.bfloat16)
        return carry

    lax.fori_loop(0, pairs, ready, 0)

    waits = jnp.where(ctx > 0, n_head - 1 + n_sub - 1, 0) + (n - 1 - ctx)
    pl.semaphore_wait(barrier, waits)

    def rows_of(slot, x, s):
        return pl.ds(pl.multiple_of(slot * rows + (x * n_sub + s) * piece, piece), piece)

    def z_copy(shard, target):
        return pltpu.make_async_remote_copy(
            keys.at[rows_of(n - 1, head, sub)], keys.at[rows_of(shard, head, sub)],
            z_send.at[target], z_recv.at[shard],
            device_id={"ctx": target}, device_id_type=MESH,
        )

    def x_copy(shard, x, step):
        where = keys.at[rows_of(shard, x, sub)]
        return pltpu.make_async_remote_copy(
            where, where, x_send.at[shard, step], x_recv.at[shard, x],
            device_id={"head": lax.rem(head + step, n_head)}, device_id_type=MESH,
        )

    def s_copy(shard, x, s, step):
        where = keys.at[rows_of(shard, x, s)]
        return pltpu.make_async_remote_copy(
            where, where, s_send.at[shard, x, step], s_recv.at[shard, x, s],
            device_id={"sub": lax.rem(sub + step, n_sub)}, device_id_type=MESH,
        )

    for target in range(n - 1, 0, -1):

        @pl.when(ctx < target)
        def _():
            z_copy(ctx, target).start()

    def project(block, pair):
        return jnp.dot(
            keys[block, pl.ds(0, width)], w_buf[pair], preferred_element_type=jnp.float32
        ).astype(jnp.bfloat16)

    def pass_on(shard):
        @pl.when(shard < ctx)
        def _():
            z_copy(shard, ctx).wait_recv()
            for step in range(1, n_head):
                x_copy(shard, head, step).start()
            for step in range(1, n_sub):
                s_copy(shard, head, sub, step).start()

    def pass_to_sibling(shard):
        @pl.when(shard < ctx)
        def _():
            for step in range(1, n_head):
                x = lax.rem(head + step, n_head)
                x_copy(shard, x, step).wait_recv()
                for s_step in range(1, n_sub):
                    s_copy(shard, x, sub, s_step).start()

    def complete(shard):
        for x in range(n_head):
            for s_step in range(1, n_sub):
                s_copy(shard, x, lax.rem(sub + s_step, n_sub), s_step).wait_recv()

    order = list(range(n - 2, -1, -1))
    if n_chunks == 1:

        def turn(pair, carry):
            w_load(pair).wait()
            for which in range(2):
                first = which * KVDIM + NOPE
                at = pl.multiple_of((2 * pair + which) * VDIM, VDIM)
                value_w[pl.ds(at, VDIM), :] = w_buf[pair, :, first : first + VDIM].T
            return carry

        half = pairs // 2
        values_t[:, pl.ds(VDIM, ONES), :] = jnp.ones((2 * pairs, ONES, chunk), jnp.bfloat16)
        lax.fori_loop(0, half, turn, 0)
        pass_on(order[0])
        lax.fori_loop(half, pairs, turn, 0)
    else:
        for pair in range(pairs):
            w_load(pair).wait()
        pass_on(order[0])
    for earlier, later in zip(order[:-1], order[1:]):
        pass_on(later)
        pass_to_sibling(earlier)
    pass_to_sibling(order[-1])
    for shard in order:

        @pl.when(shard < ctx)
        def _():
            complete(shard)

    length = length_ref[0]
    row_pos = ctx * rows + lax.broadcasted_iota(jnp.int32, (rows, 1), 0)
    last_key = jnp.minimum(row_pos, length - 1)
    live = row_pos < length

    def allowed_keys(first):
        slot_pos = first + lax.broadcasted_iota(jnp.int32, (1, chunk), 1)
        far = n * rows
        position = jnp.where(
            slot_pos >= others, slot_pos - others + ctx * rows, jnp.where(slot_pos < ctx * rows, slot_pos, far)
        )
        return position <= last_key

    def head_scores(pair, which, key_nope, key_rope, allowed):
        k = jnp.concatenate([key_nope, key_rope], 1)
        scores = lax.dot_general(
            q_ready[2 * pair + which], k, (((1,), (1,)), ((), ())), preferred_element_type=jnp.float32
        )
        return jnp.where(allowed, scores, -1e30)

    def head_mix(weights, values):
        v = jnp.concatenate([values, jnp.ones_like(values)], 1)
        return jnp.dot(weights.astype(jnp.bfloat16), v, preferred_element_type=jnp.float32)

    def finish(pair, which, mixed):
        result = jnp.where(live, mixed[:, :VDIM] / mixed[:, VDIM:], 0.0)
        at = pl.multiple_of((2 * pair + which) * VDIM, VDIM)
        out[:, pl.ds(at, VDIM)] = result.astype(jnp.bfloat16)

    if n_chunks == 1:
        group = pairs
        column = lax.broadcasted_iota(jnp.int32, (1, rows), 1) + ctx * rows
        slot_pos = lax.broadcasted_iota(jnp.int32, (chunk, 1), 0)
        key_pos = jnp.where(
            slot_pos >= others, slot_pos - others + ctx * rows,
            jnp.where(slot_pos < ctx * rows, slot_pos, n * rows),
        )
        allowed = key_pos <= jnp.minimum(column, length - 1)
        live_t = column < length

        for part in range(2 * pairs // group):
            spread = lax.dot_general(
                value_w[pl.ds(part * group * VDIM, group * VDIM), :], keys[:, pl.ds(0, width)],
                (((1,), (1,)), ((), ())), preferred_element_type=jnp.float32,
            ).astype(jnp.bfloat16)
            values_t[pl.ds(part * group, group), pl.ds(0, VDIM), :] = spread.reshape(group, VDIM, chunk)

        def attend(pair, carry):
            key_w = jnp.concatenate(
                [w_buf[pair, :, which * KVDIM : which * KVDIM + NOPE] for which in range(2)], 1
            )
            key_nope = jnp.dot(
                keys[:, pl.ds(0, width)], key_w, preferred_element_type=jnp.float32
            ).astype(jnp.bfloat16)
            key_rope = keys[:, pl.ds(width, 2 * ROPE)]
            for which in range(2):
                k = jnp.concatenate([key_nope[:, which * NOPE : (which + 1) * NOPE], key_rope], 1)
                scores = lax.dot_general(
                    k, q_ready[2 * pair + which], (((1,), (1,)), ((), ())),
                    preferred_element_type=jnp.float32,
                )
                scores = jnp.where(allowed, scores, -1e30)
                top = jnp.max(scores, 0, keepdims=True)
                weights = jnp.exp2((scores - top) * SCORE_SCALE).astype(jnp.bfloat16)
                mixed = jnp.dot(
                    values_t[2 * pair + which], weights, preferred_element_type=jnp.float32
                )
                result = jnp.where(live_t, mixed[:VDIM] / mixed[VDIM : VDIM + 1], 0.0)
                at = pl.multiple_of((2 * pair + which) * VDIM, VDIM)
                out[:, pl.ds(at, VDIM)] = result.T.astype(jnp.bfloat16)
            return carry

        lax.fori_loop(0, pairs, attend, 0, unroll=2)
    else:

        def attend(pair, carry):
            needed = jnp.minimum((ctx * rows + chunk - 1) // chunk, n_chunks - 1)

            def one_chunk(step, state):
                index = jnp.where(step == needed, n_chunks - 1, step)
                at = pl.multiple_of(index * chunk, chunk)
                block = pl.ds(at, chunk)
                expanded = project(block, pair)
                allowed = allowed_keys(at)
                later = []
                for which in range(2):
                    top, mixed = state[which]
                    first = which * KVDIM
                    scores = head_scores(
                        pair, which, expanded[:, first : first + NOPE],
                        keys[block, pl.ds(width, 2 * ROPE)], allowed,
                    )
                    new_top = jnp.maximum(top, jnp.max(scores, -1, keepdims=True))
                    weights = jnp.where(allowed, jnp.exp2((scores - new_top) * SCORE_SCALE), 0.0)
                    fade = jnp.exp2((top - new_top) * SCORE_SCALE)
                    mix = head_mix(weights, expanded[:, first + NOPE : first + KVDIM])
                    later.append((new_top, mixed * fade + mix))
                return tuple(later)

            blank = (jnp.full((rows, 1), -1e30, jnp.float32), jnp.zeros((rows, 2 * VDIM), jnp.float32))
            state = lax.fori_loop(0, needed + 1, one_chunk, (blank, blank))
            for which in range(2):
                finish(pair, which, state[which][1])
            return carry

        lax.fori_loop(0, pairs, attend, 0)

    for target in range(n - 1, 0, -1):

        @pl.when(ctx < target)
        def _():
            z_copy(ctx, target).wait_send()

    for shard in range(n - 2, -1, -1):

        @pl.when(shard < ctx)
        def _():
            for step in range(1, n_head):
                x_copy(shard, head, step).wait_send()
            for step in range(1, n_sub):
                for x in range(n_head):
                    s_copy(shard, x, sub, step).wait_send()


def per_device(n, n_head, n_sub, queries, latent, rope_keys, latent_gain, up_weight, prompt_length):
    rows, width = latent.shape
    pairs = up_weight.shape[1] // (2 * KVDIM)
    heads = 2 * pairs
    tokens = n * rows
    chunk = tokens if tokens <= 512 else (512 if tokens % 512 == 0 else rows)
    anywhere = pl.BlockSpec(memory_space=pl.ANY)
    dma = pltpu.SemaphoreType.DMA
    cost = pl.CostEstimate(
        flops=2 * tokens * width * up_weight.shape[1] + 2 * heads * rows * tokens * (QDIM + VDIM),
        bytes_accessed=2 * (queries.size + up_weight.size + rows * heads * VDIM),
        transcendentals=heads * rows * tokens,
    )
    return pl.pallas_call(
        functools.partial(kernel, n, n_head, n_sub, chunk),
        out_shape=pltpu.VMEM((rows, heads * VDIM), jnp.bfloat16),
        in_specs=[pl.BlockSpec(memory_space=pltpu.SMEM)] + [anywhere] * 5,
        out_specs=pl.BlockSpec(memory_space=pltpu.VMEM),
        scratch_shapes=[
            pltpu.VMEM((tokens, width + 2 * ROPE), jnp.bfloat16),
            pltpu.VMEM(queries.shape, jnp.bfloat16),
            pltpu.VMEM((heads, rows, NOPE + 2 * ROPE), jnp.bfloat16),
            pltpu.VMEM((pairs, width, 2 * KVDIM), jnp.bfloat16),
            pltpu.VMEM((heads * VDIM, width), jnp.bfloat16),
            pltpu.VMEM((heads, VDIM + ONES, chunk), jnp.bfloat16),
            pltpu.VMEM((rows, width), jnp.bfloat16),
            pltpu.VMEM((ROPE, rows), jnp.bfloat16),
            pltpu.VMEM((width,), jnp.float32),
            dma((4,)),
            dma((pairs,)),
            dma((n,)),
            dma((n,)),
            dma((n, n_head)),
            dma((n, n_head)),
            dma((n, n_head, n_sub)),
            dma((n, n_head, n_sub)),
        ],
        compiler_params=pltpu.CompilerParams(
            collective_id=0, has_side_effects=True, vmem_limit_bytes=63 * 1024 * 1024
        ),
        cost_estimate=cost,
        name="mla_prefill",
    )(prompt_length, queries, latent, rope_keys.T, latent_gain, up_weight)


def solution(mesh):
    placed = (
        P(("parts", "ctx"), ("head", "sub")),
        P(("parts", "ctx"), None),
        P(("parts", "ctx"), None),
        P(),
        P(None, ("head", "sub")),
        P("parts"),
    )
    return jax.shard_map(
        functools.partial(per_device, mesh.shape["ctx"], mesh.shape["head"], mesh.shape["sub"]),
        mesh=mesh,
        in_specs=placed,
        out_specs=P(("parts", "ctx"), ("head", "sub")),
        check_vma=False,
    )
```

```python
import functools
import math

import jax
import jax.numpy as jnp
from jax import lax
from jax.experimental import pallas as pl
from jax.experimental.pallas import tpu as pltpu
from jax.sharding import PartitionSpec as P

ROPE = 64
NOPE = 128
VDIM = 128
QDIM = NOPE + ROPE
KVDIM = NOPE + VDIM
MESH = pl.DeviceIdType.MESH
SCORE_SCALE = math.log2(math.e) / math.sqrt(NOPE + ROPE)


def angle_tables(first_pos, rows):
    lane8 = lax.broadcasted_iota(jnp.int32, (8, 2 * ROPE), 1)
    half = ROPE // 2
    frequency = jnp.exp((lane8 % half).astype(jnp.float32) * (-math.log(10000.0) / half))
    low = lax.broadcasted_iota(jnp.int32, (8, 2 * ROPE), 0).astype(jnp.float32) * frequency
    blocks = rows // 8
    lane = lax.broadcasted_iota(jnp.int32, (blocks, 2 * ROPE), 1)
    block_frequency = jnp.exp((lane % half).astype(jnp.float32) * (-math.log(10000.0) / half))
    base = (first_pos + 8 * lax.broadcasted_iota(jnp.int32, (blocks, 2 * ROPE), 0)).astype(jnp.float32)
    high = base * block_frequency
    cos_low, sin_low = jnp.cos(low), jnp.sin(low)
    cos_high, sin_high = jnp.cos(high), jnp.sin(high)
    cosines, sines = [], []
    for block in range(blocks):
        ch, sh = cos_high[block : block + 1], sin_high[block : block + 1]
        cosines.append(ch * cos_low - sh * sin_low)
        sines.append(sh * cos_low + ch * sin_low)
    cosine = jnp.concatenate(cosines, 0)
    sine = jnp.concatenate(sines, 0)
    lane = lax.broadcasted_iota(jnp.int32, (rows, 2 * ROPE), 1)
    return cosine, jnp.where(lane % ROPE < half, -sine, sine)


def rotate_pair(values, cosine, sine):
    half = ROPE // 2
    lane = lax.broadcasted_iota(jnp.int32, values.shape, 1)
    swapped = jnp.where(
        lane % ROPE < half, pltpu.roll(values, 2 * ROPE - half, 1), pltpu.roll(values, half, 1)
    )
    return values * cosine + swapped * sine


def kernel(
    n, n_head, n_sub, chunk,
    length_ref, queries, latent, rope_keys, latent_gain, up_weight, out,
    keys, q_raw, q_ready, w_buf, kv, own_top, own_mix, lat_buf, rope_buf, gain_buf,
    load_sem, w_sem, z_send, z_recv, x_send, x_recv, s_send, s_recv,
):
    ctx = lax.axis_index("ctx")
    head = lax.axis_index("head")
    sub = lax.axis_index("sub")
    rows = latent.shape[0]
    width = latent.shape[1]
    pairs = w_buf.shape[0]
    pair_w = 2 * KVDIM
    pair_q = 2 * QDIM
    piece = rows // (n_head * n_sub)
    others = (n - 1) * rows
    n_chunks = n * rows // chunk

    loads = [
        pltpu.make_async_copy(latent, lat_buf, load_sem.at[0]),
        pltpu.make_async_copy(rope_keys, rope_buf, load_sem.at[1]),
        pltpu.make_async_copy(latent_gain, gain_buf, load_sem.at[2]),
        pltpu.make_async_copy(queries, q_raw, load_sem.at[3]),
    ]
    for load in loads:
        load.start()

    def w_load(pair):
        return pltpu.make_async_copy(
            up_weight.at[:, pl.ds(pl.multiple_of(pair * pair_w, pair_w), pair_w)],
            w_buf.at[pair],
            w_sem.at[pair],
        )

    for pair in range(pairs):
        w_load(pair).start()

    barrier = pltpu.get_barrier_semaphore()
    for other in range(n - 1):

        @pl.when(other < ctx)
        def _():
            pl.semaphore_signal(barrier, inc=1, device_id={"ctx": other}, device_id_type=MESH)

    @pl.when(ctx > 0)
    def _():
        for step in range(1, n_head):
            pl.semaphore_signal(
                barrier, inc=1, device_id={"head": lax.rem(head + step, n_head)}, device_id_type=MESH
            )
        for step in range(1, n_sub):
            pl.semaphore_signal(
                barrier, inc=1, device_id={"sub": lax.rem(sub + step, n_sub)}, device_id_type=MESH
            )

    cosine, sine = angle_tables(ctx * rows, rows)

    loads[0].wait()
    loads[1].wait()
    loads[2].wait()
    widened = lat_buf[...].astype(jnp.float32)
    mean = jnp.mean(widened * widened, -1, keepdims=True)
    normed = (widened * lax.rsqrt(mean + 1e-06) * gain_buf[...].reshape(1, width)).astype(jnp.bfloat16)
    rope = rope_buf[...].astype(jnp.float32)
    rope = jnp.concatenate([rope, rope], 0).T
    rotated = rotate_pair(rope, cosine, sine).astype(jnp.bfloat16)
    own = pl.ds(others, rows)
    keys[own, pl.ds(0, width)] = normed
    keys[own, pl.ds(width, 2 * ROPE)] = rotated

    for slot in range(n - 1):

        @pl.when(ctx <= slot)
        def _():
            keys[pl.ds(slot * rows, rows), :] = jnp.zeros((rows, width + 2 * ROPE), jnp.bfloat16)

    loads[3].wait()
    lane = lax.broadcasted_iota(jnp.int32, (rows, 2 * ROPE), 1)
    lower = lane < ROPE

    def ready(pair, carry):
        at = pl.multiple_of(pair * pair_q, 128)
        tile1 = q_raw[:, pl.ds(at + NOPE, 128)].astype(jnp.float32)
        tile2 = q_raw[:, pl.ds(at + 2 * NOPE, 128)].astype(jnp.float32)
        spun = rotate_pair(jnp.where(lower, tile1, tile2), cosine, sine)
        q_ready[2 * pair, :, :NOPE] = q_raw[:, pl.ds(at, NOPE)]
        q_ready[2 * pair, :, NOPE:] = jnp.where(lower, spun, 0.0).astype(jnp.bfloat16)
        q_ready[2 * pair + 1, :, :NOPE] = pltpu.roll(
            jnp.where(lower, tile2, tile1), ROPE, 1
        ).astype(jnp.bfloat16)
        q_ready[2 * pair + 1, :, NOPE:] = jnp.where(lower, 0.0, spun).astype(jnp.bfloat16)
        return carry

    lax.fori_loop(0, pairs, ready, 0)

    waits = jnp.where(ctx > 0, n_head - 1 + n_sub - 1, 0) + (n - 1 - ctx)
    pl.semaphore_wait(barrier, waits)

    def rows_of(slot, x, s):
        return pl.ds(pl.multiple_of(slot * rows + (x * n_sub + s) * piece, piece), piece)

    def z_copy(shard, target):
        return pltpu.make_async_remote_copy(
            keys.at[rows_of(n - 1, head, sub)], keys.at[rows_of(shard, head, sub)],
            z_send.at[target], z_recv.at[shard],
            device_id={"ctx": target}, device_id_type=MESH,
        )

    def x_copy(shard, x, step):
        where = keys.at[rows_of(shard, x, sub)]
        return pltpu.make_async_remote_copy(
            where, where, x_send.at[shard, step], x_recv.at[shard, x],
            device_id={"head": lax.rem(head + step, n_head)}, device_id_type=MESH,
        )

    def s_copy(shard, x, s, step):
        where = keys.at[rows_of(shard, x, s)]
        return pltpu.make_async_remote_copy(
            where, where, s_send.at[shard, x, step], s_recv.at[shard, x, s],
            device_id={"sub": lax.rem(sub + step, n_sub)}, device_id_type=MESH,
        )

    for target in range(n - 1, 0, -1):

        @pl.when(ctx < target)
        def _():
            z_copy(ctx, target).start()

    def project(block, pair):
        return jnp.dot(
            keys[block, pl.ds(0, width)], w_buf[pair], preferred_element_type=jnp.float32
        ).astype(jnp.bfloat16)

    def pass_on(shard):
        @pl.when(shard < ctx)
        def _():
            z_copy(shard, ctx).wait_recv()
            for step in range(1, n_head):
                x_copy(shard, head, step).start()
            for step in range(1, n_sub):
                s_copy(shard, head, sub, step).start()

    def pass_to_sibling(shard):
        @pl.when(shard < ctx)
        def _():
            for step in range(1, n_head):
                x = lax.rem(head + step, n_head)
                x_copy(shard, x, step).wait_recv()
                for s_step in range(1, n_sub):
                    s_copy(shard, x, sub, s_step).start()

    def complete(shard):
        for x in range(n_head):
            for s_step in range(1, n_sub):
                s_copy(shard, x, lax.rem(sub + s_step, n_sub), s_step).wait_recv()

    length = length_ref[0]
    row_pos = ctx * rows + lax.broadcasted_iota(jnp.int32, (rows, 1), 0)
    last_key = jnp.minimum(row_pos, length - 1)
    live = row_pos < length

    def allowed_keys(first, count):
        slot_pos = first + lax.broadcasted_iota(jnp.int32, (1, count), 1)
        far = n * rows
        position = jnp.where(
            slot_pos >= others, slot_pos - others + ctx * rows, jnp.where(slot_pos < ctx * rows, slot_pos, far)
        )
        return position <= last_key

    def head_scores(pair, which, key_nope, key_rope, allowed):
        k = jnp.concatenate([key_nope, key_rope], 1)
        scores = lax.dot_general(
            q_ready[2 * pair + which], k, (((1,), (1,)), ((), ())), preferred_element_type=jnp.float32
        )
        return jnp.where(allowed, scores, -1e30)

    def head_mix(weights, values):
        v = jnp.concatenate([values, jnp.ones_like(values)], 1)
        return jnp.dot(weights.astype(jnp.bfloat16), v, preferred_element_type=jnp.float32)

    def finish(pair, which, mixed):
        result = jnp.where(live, mixed[:, :VDIM] / mixed[:, VDIM:], 0.0)
        at = pl.multiple_of((2 * pair + which) * VDIM, VDIM)
        out[:, pl.ds(at, VDIM)] = result.astype(jnp.bfloat16)

    def own_part(pair, carry):
        w_load(pair).wait()
        expanded = project(own, pair)
        allowed = allowed_keys(others, rows)
        for which in range(2):
            first = which * KVDIM
            scores = head_scores(
                pair, which, expanded[:, first : first + NOPE], keys[own, pl.ds(width, 2 * ROPE)], allowed
            )
            top = jnp.max(scores, -1, keepdims=True)
            weights = jnp.exp2((scores - top) * SCORE_SCALE)
            own_top[2 * pair + which] = jnp.broadcast_to(top, (rows, VDIM))
            own_mix[2 * pair + which] = head_mix(weights, expanded[:, first + NOPE : first + KVDIM])
        return carry

    order = list(range(n - 2, -1, -1))
    bounds = [pairs * k // n for k in range(n + 1)]
    for k in range(n):
        if n_chunks == 1:
            lax.fori_loop(bounds[k], bounds[k + 1], own_part, 0, unroll=True)
        else:
            for pair in range(bounds[k], bounds[k + 1]):
                w_load(pair).wait()
        if k < n - 1:
            pass_on(order[k])
        if k > 0:
            pass_to_sibling(order[k - 1])
    for shard in order:

        @pl.when(shard < ctx)
        def _():
            complete(shard)

    if n_chunks == 1:
        allowed = allowed_keys(0, others)
        earlier = pl.ds(0, others)

        def expand(pair, carry):
            kv[pair] = project(earlier, pair)
            return carry

        lax.fori_loop(0, pairs, expand, 0, unroll=2)

        def attend(pair, carry):
            scores = [
                head_scores(
                    pair, which, kv[pair, :, which * KVDIM : which * KVDIM + NOPE],
                    keys[earlier, pl.ds(width, 2 * ROPE)], allowed,
                )
                for which in range(2)
            ]
            for which in range(2):
                before = own_top[2 * pair + which][:, :1]
                top = jnp.maximum(before, jnp.max(scores[which], -1, keepdims=True))
                weights = jnp.exp2((scores[which] - top) * SCORE_SCALE)
                fade = jnp.exp2((before - top) * SCORE_SCALE)
                mixed = head_mix(weights, kv[pair, :, which * KVDIM + NOPE : (which + 1) * KVDIM])
                finish(pair, which, mixed + own_mix[2 * pair + which] * fade)
            return carry

        lax.fori_loop(0, pairs, attend, 0, unroll=2)
    else:

        def attend(pair, carry):
            needed = jnp.minimum((ctx * rows + chunk - 1) // chunk, n_chunks - 1)

            def one_chunk(step, state):
                index = jnp.where(step == needed, n_chunks - 1, step)
                at = pl.multiple_of(index * chunk, chunk)
                block = pl.ds(at, chunk)
                expanded = project(block, pair)
                allowed = allowed_keys(at, chunk)
                later = []
                for which in range(2):
                    top, mixed = state[which]
                    first = which * KVDIM
                    scores = head_scores(
                        pair, which, expanded[:, first : first + NOPE],
                        keys[block, pl.ds(width, 2 * ROPE)], allowed,
                    )
                    new_top = jnp.maximum(top, jnp.max(scores, -1, keepdims=True))
                    weights = jnp.where(allowed, jnp.exp2((scores - new_top) * SCORE_SCALE), 0.0)
                    fade = jnp.exp2((top - new_top) * SCORE_SCALE)
                    mix = head_mix(weights, expanded[:, first + NOPE : first + KVDIM])
                    later.append((new_top, mixed * fade + mix))
                return tuple(later)

            blank = (jnp.full((rows, 1), -1e30, jnp.float32), jnp.zeros((rows, 2 * VDIM), jnp.float32))
            state = lax.fori_loop(0, needed + 1, one_chunk, (blank, blank))
            for which in range(2):
                finish(pair, which, state[which][1])
            return carry

        lax.fori_loop(0, pairs, attend, 0)

    for target in range(n - 1, 0, -1):

        @pl.when(ctx < target)
        def _():
            z_copy(ctx, target).wait_send()

    for shard in range(n - 2, -1, -1):

        @pl.when(shard < ctx)
        def _():
            for step in range(1, n_head):
                x_copy(shard, head, step).wait_send()
            for step in range(1, n_sub):
                for x in range(n_head):
                    s_copy(shard, x, sub, step).wait_send()


def per_device(n, n_head, n_sub, queries, latent, rope_keys, latent_gain, up_weight, prompt_length):
    rows, width = latent.shape
    pairs = up_weight.shape[1] // (2 * KVDIM)
    heads = 2 * pairs
    tokens = n * rows
    chunk = tokens if tokens <= 512 else (512 if tokens % 512 == 0 else rows)
    anywhere = pl.BlockSpec(memory_space=pl.ANY)
    dma = pltpu.SemaphoreType.DMA
    cost = pl.CostEstimate(
        flops=2 * tokens * width * up_weight.shape[1] + 2 * heads * rows * tokens * (QDIM + VDIM),
        bytes_accessed=2 * (queries.size + up_weight.size + rows * heads * VDIM),
        transcendentals=heads * rows * tokens,
    )
    return pl.pallas_call(
        functools.partial(kernel, n, n_head, n_sub, chunk),
        out_shape=pltpu.VMEM((rows, heads * VDIM), jnp.bfloat16),
        in_specs=[pl.BlockSpec(memory_space=pltpu.SMEM)] + [anywhere] * 5,
        out_specs=pl.BlockSpec(memory_space=pltpu.VMEM),
        scratch_shapes=[
            pltpu.VMEM((tokens, width + 2 * ROPE), jnp.bfloat16),
            pltpu.VMEM(queries.shape, jnp.bfloat16),
            pltpu.VMEM((heads, rows, NOPE + 2 * ROPE), jnp.bfloat16),
            pltpu.VMEM((pairs, width, 2 * KVDIM), jnp.bfloat16),
            pltpu.VMEM((pairs, chunk - rows if chunk == tokens else 16, 2 * KVDIM), jnp.bfloat16),
            pltpu.VMEM((heads, rows, VDIM), jnp.float32),
            pltpu.VMEM((heads, rows, 2 * VDIM), jnp.float32),
            pltpu.VMEM((rows, width), jnp.bfloat16),
            pltpu.VMEM((ROPE, rows), jnp.bfloat16),
            pltpu.VMEM((width,), jnp.float32),
            dma((4,)),
            dma((pairs,)),
            dma((n,)),
            dma((n,)),
            dma((n, n_head)),
            dma((n, n_head)),
            dma((n, n_head, n_sub)),
            dma((n, n_head, n_sub)),
        ],
        compiler_params=pltpu.CompilerParams(
            collective_id=0, has_side_effects=True, vmem_limit_bytes=63 * 1024 * 1024
        ),
        cost_estimate=cost,
        name="mla_prefill",
    )(prompt_length, queries, latent, rope_keys.T, latent_gain, up_weight)


def solution(mesh):
    placed = (
        P(("parts", "ctx"), ("head", "sub")),
        P(("parts", "ctx"), None),
        P(("parts", "ctx"), None),
        P(),
        P(None, ("head", "sub")),
        P("parts"),
    )
    return jax.shard_map(
        functools.partial(per_device, mesh.shape["ctx"], mesh.shape["head"], mesh.shape["sub"]),
        mesh=mesh,
        in_specs=placed,
        out_specs=P(("parts", "ctx"), ("head", "sub")),
        check_vma=False,
    )
```

```python
import functools
import math

import jax
import jax.numpy as jnp
from jax import lax
from jax.experimental import pallas as pl
from jax.experimental.pallas import tpu as pltpu
from jax.sharding import PartitionSpec as P

ROPE = 64
NOPE = 128
VDIM = 128
QDIM = NOPE + ROPE
KVDIM = NOPE + VDIM
MESH = pl.DeviceIdType.MESH
SCORE_SCALE = math.log2(math.e) / math.sqrt(NOPE + ROPE)


def angle_tables(first_pos, rows):
    lane8 = lax.broadcasted_iota(jnp.int32, (8, 2 * ROPE), 1)
    half = ROPE // 2
    frequency = jnp.exp((lane8 % half).astype(jnp.float32) * (-math.log(10000.0) / half))
    low = lax.broadcasted_iota(jnp.int32, (8, 2 * ROPE), 0).astype(jnp.float32) * frequency
    blocks = rows // 8
    lane = lax.broadcasted_iota(jnp.int32, (blocks, 2 * ROPE), 1)
    block_frequency = jnp.exp((lane % half).astype(jnp.float32) * (-math.log(10000.0) / half))
    base = (first_pos + 8 * lax.broadcasted_iota(jnp.int32, (blocks, 2 * ROPE), 0)).astype(jnp.float32)
    high = base * block_frequency
    cos_low, sin_low = jnp.cos(low), jnp.sin(low)
    cos_high, sin_high = jnp.cos(high), jnp.sin(high)
    cosines, sines = [], []
    for block in range(blocks):
        ch, sh = cos_high[block : block + 1], sin_high[block : block + 1]
        cosines.append(ch * cos_low - sh * sin_low)
        sines.append(sh * cos_low + ch * sin_low)
    cosine = jnp.concatenate(cosines, 0)
    sine = jnp.concatenate(sines, 0)
    lane = lax.broadcasted_iota(jnp.int32, (rows, 2 * ROPE), 1)
    return cosine, jnp.where(lane % ROPE < half, -sine, sine)


def rotate_pair(values, cosine, sine):
    half = ROPE // 2
    lane = lax.broadcasted_iota(jnp.int32, values.shape, 1)
    swapped = jnp.where(
        lane % ROPE < half, pltpu.roll(values, 2 * ROPE - half, 1), pltpu.roll(values, half, 1)
    )
    return values * cosine + swapped * sine


def kernel(
    n, n_head, n_sub, chunk,
    length_ref, queries, latent, rope_keys, latent_gain, up_weight, out,
    keys, q_raw, q_ready, w_buf, kv, lat_buf, rope_buf, gain_buf,
    load_sem, w_sem, z_send, z_recv, x_send, x_recv, s_send, s_recv,
):
    ctx = lax.axis_index("ctx")
    head = lax.axis_index("head")
    sub = lax.axis_index("sub")
    rows = latent.shape[0]
    width = latent.shape[1]
    pairs = w_buf.shape[0]
    pair_w = 2 * KVDIM
    pair_q = 2 * QDIM
    piece = rows // (n_head * n_sub)
    others = (n - 1) * rows
    n_chunks = n * rows // chunk

    loads = [
        pltpu.make_async_copy(latent, lat_buf, load_sem.at[0]),
        pltpu.make_async_copy(rope_keys, rope_buf, load_sem.at[1]),
        pltpu.make_async_copy(latent_gain, gain_buf, load_sem.at[2]),
        pltpu.make_async_copy(queries, q_raw, load_sem.at[3]),
    ]
    for load in loads:
        load.start()

    def w_load(pair):
        return pltpu.make_async_copy(
            up_weight.at[:, pl.ds(pl.multiple_of(pair * pair_w, pair_w), pair_w)],
            w_buf.at[pair],
            w_sem.at[pair],
        )

    for pair in range(pairs):
        w_load(pair).start()

    barrier = pltpu.get_barrier_semaphore()
    for other in range(n - 1):

        @pl.when(other < ctx)
        def _():
            pl.semaphore_signal(barrier, inc=1, device_id={"ctx": other}, device_id_type=MESH)

    @pl.when(ctx > 0)
    def _():
        for step in range(1, n_head):
            pl.semaphore_signal(
                barrier, inc=1, device_id={"head": lax.rem(head + step, n_head)}, device_id_type=MESH
            )
        for step in range(1, n_sub):
            pl.semaphore_signal(
                barrier, inc=1, device_id={"sub": lax.rem(sub + step, n_sub)}, device_id_type=MESH
            )

    cosine, sine = angle_tables(ctx * rows, rows)

    loads[0].wait()
    loads[1].wait()
    loads[2].wait()
    widened = lat_buf[...].astype(jnp.float32)
    mean = jnp.mean(widened * widened, -1, keepdims=True)
    normed = (widened * lax.rsqrt(mean + 1e-06) * gain_buf[...].reshape(1, width)).astype(jnp.bfloat16)
    rope = rope_buf[...].astype(jnp.float32)
    rope = jnp.concatenate([rope, rope], 0).T
    rotated = rotate_pair(rope, cosine, sine).astype(jnp.bfloat16)
    own = pl.ds(others, rows)
    keys[own, pl.ds(0, width)] = normed
    keys[own, pl.ds(width, 2 * ROPE)] = rotated

    for slot in range(n - 1):

        @pl.when(ctx <= slot)
        def _():
            keys[pl.ds(slot * rows, rows), :] = jnp.zeros((rows, width + 2 * ROPE), jnp.bfloat16)

    loads[3].wait()
    lane = lax.broadcasted_iota(jnp.int32, (rows, 2 * ROPE), 1)
    lower = lane < ROPE

    def ready(pair, carry):
        at = pl.multiple_of(pair * pair_q, 128)
        tile1 = q_raw[:, pl.ds(at + NOPE, 128)].astype(jnp.float32)
        tile2 = q_raw[:, pl.ds(at + 2 * NOPE, 128)].astype(jnp.float32)
        spun = rotate_pair(jnp.where(lower, tile1, tile2), cosine, sine)
        q_ready[2 * pair, :, :NOPE] = q_raw[:, pl.ds(at, NOPE)]
        q_ready[2 * pair, :, NOPE:] = jnp.where(lower, spun, 0.0).astype(jnp.bfloat16)
        q_ready[2 * pair + 1, :, :NOPE] = pltpu.roll(
            jnp.where(lower, tile2, tile1), ROPE, 1
        ).astype(jnp.bfloat16)
        q_ready[2 * pair + 1, :, NOPE:] = jnp.where(lower, 0.0, spun).astype(jnp.bfloat16)
        return carry

    lax.fori_loop(0, pairs, ready, 0)

    waits = jnp.where(ctx > 0, n_head - 1 + n_sub - 1, 0) + (n - 1 - ctx)
    pl.semaphore_wait(barrier, waits)

    def rows_of(slot, x, s):
        return pl.ds(pl.multiple_of(slot * rows + (x * n_sub + s) * piece, piece), piece)

    def z_copy(shard, target):
        return pltpu.make_async_remote_copy(
            keys.at[rows_of(n - 1, head, sub)], keys.at[rows_of(shard, head, sub)],
            z_send.at[target], z_recv.at[shard],
            device_id={"ctx": target}, device_id_type=MESH,
        )

    def x_copy(shard, x, step):
        where = keys.at[rows_of(shard, x, sub)]
        return pltpu.make_async_remote_copy(
            where, where, x_send.at[shard, step], x_recv.at[shard, x],
            device_id={"head": lax.rem(head + step, n_head)}, device_id_type=MESH,
        )

    def s_copy(shard, x, s, step):
        where = keys.at[rows_of(shard, x, s)]
        return pltpu.make_async_remote_copy(
            where, where, s_send.at[shard, x, step], s_recv.at[shard, x, s],
            device_id={"sub": lax.rem(sub + step, n_sub)}, device_id_type=MESH,
        )

    for target in range(n - 1, 0, -1):

        @pl.when(ctx < target)
        def _():
            z_copy(ctx, target).start()

    def project(block, pair):
        return jnp.dot(
            keys[block, pl.ds(0, width)], w_buf[pair], preferred_element_type=jnp.float32
        ).astype(jnp.bfloat16)

    def expand(block, fresh):
        def one(pair, carry):
            if fresh:
                w_load(pair).wait()
            kv[pair, block, :] = project(block, pair)
            return carry

        lax.fori_loop(0, pairs, one, 0, unroll=2)

    def pass_on(shard):
        @pl.when(shard < ctx)
        def _():
            z_copy(shard, ctx).wait_recv()
            for step in range(1, n_head):
                x_copy(shard, head, step).start()
            for step in range(1, n_sub):
                s_copy(shard, head, sub, step).start()

    def pass_to_sibling(shard):
        @pl.when(shard < ctx)
        def _():
            for step in range(1, n_head):
                x = lax.rem(head + step, n_head)
                x_copy(shard, x, step).wait_recv()
                for s_step in range(1, n_sub):
                    s_copy(shard, x, sub, s_step).start()

    def complete(shard):
        for x in range(n_head):
            for s_step in range(1, n_sub):
                s_copy(shard, x, lax.rem(sub + s_step, n_sub), s_step).wait_recv()

    order = list(range(n - 2, -1, -1))
    if n_chunks == 1:
        expand(own, True)
    else:
        for pair in range(pairs):
            w_load(pair).wait()
    pass_on(order[0])
    for earlier, later in zip(order[:-1], order[1:]):
        pass_on(later)
        pass_to_sibling(earlier)
    pass_to_sibling(order[-1])
    for shard in order:

        @pl.when(shard < ctx)
        def _():
            complete(shard)

    length = length_ref[0]
    row_pos = ctx * rows + lax.broadcasted_iota(jnp.int32, (rows, 1), 0)
    last_key = jnp.minimum(row_pos, length - 1)
    live = row_pos < length

    def allowed_keys(first):
        slot_pos = first + lax.broadcasted_iota(jnp.int32, (1, chunk), 1)
        far = n * rows
        position = jnp.where(
            slot_pos >= others, slot_pos - others + ctx * rows, jnp.where(slot_pos < ctx * rows, slot_pos, far)
        )
        return position <= last_key

    def head_scores(pair, which, key_nope, key_rope, allowed):
        k = jnp.concatenate([key_nope, key_rope], 1)
        scores = lax.dot_general(
            q_ready[2 * pair + which], k, (((1,), (1,)), ((), ())), preferred_element_type=jnp.float32
        )
        return jnp.where(allowed, scores, -1e30)

    def head_mix(weights, values):
        v = jnp.concatenate([values, jnp.ones_like(values)], 1)
        return jnp.dot(weights.astype(jnp.bfloat16), v, preferred_element_type=jnp.float32)

    def finish(pair, which, mixed):
        result = jnp.where(live, mixed[:, :VDIM] / mixed[:, VDIM:], 0.0)
        at = pl.multiple_of((2 * pair + which) * VDIM, VDIM)
        out[:, pl.ds(at, VDIM)] = result.astype(jnp.bfloat16)

    if n_chunks == 1:
        allowed = allowed_keys(0)

        expand(pl.ds(0, others), False)
        together = 4 if pairs % 2 == 0 else 2

        def attend(step, carry):
            where = [(step * (together // 2) + k // 2, k % 2) for k in range(together)]
            key_rope = keys[:, pl.ds(width, 2 * ROPE)]
            scores = [
                head_scores(
                    pair, which, kv[pair, :, which * KVDIM : which * KVDIM + NOPE], key_rope, allowed
                )
                for pair, which in where
            ]
            tops = [jnp.max(score, -1, keepdims=True) for score in scores]
            weights = [
                jnp.exp2((score - top) * SCORE_SCALE).astype(jnp.bfloat16)
                for score, top in zip(scores, tops)
            ]
            mixes = [
                head_mix(weight, kv[pair, :, which * KVDIM + NOPE : (which + 1) * KVDIM])
                for (pair, which), weight in zip(where, weights)
            ]
            for (pair, which), mixed in zip(where, mixes):
                finish(pair, which, mixed)
            return carry

        lax.fori_loop(0, 2 * pairs // together, attend, 0)
    else:

        def attend(pair, carry):
            needed = jnp.minimum((ctx * rows + chunk - 1) // chunk, n_chunks - 1)

            def one_chunk(step, state):
                index = jnp.where(step == needed, n_chunks - 1, step)
                at = pl.multiple_of(index * chunk, chunk)
                block = pl.ds(at, chunk)
                expanded = project(block, pair)
                allowed = allowed_keys(at)
                later = []
                for which in range(2):
                    top, mixed = state[which]
                    first = which * KVDIM
                    scores = head_scores(
                        pair, which, expanded[:, first : first + NOPE],
                        keys[block, pl.ds(width, 2 * ROPE)], allowed,
                    )
                    new_top = jnp.maximum(top, jnp.max(scores, -1, keepdims=True))
                    weights = jnp.where(allowed, jnp.exp2((scores - new_top) * SCORE_SCALE), 0.0)
                    fade = jnp.exp2((top - new_top) * SCORE_SCALE)
                    mix = head_mix(weights, expanded[:, first + NOPE : first + KVDIM])
                    later.append((new_top, mixed * fade + mix))
                return tuple(later)

            blank = (jnp.full((rows, 1), -1e30, jnp.float32), jnp.zeros((rows, 2 * VDIM), jnp.float32))
            state = lax.fori_loop(0, needed + 1, one_chunk, (blank, blank))
            for which in range(2):
                finish(pair, which, state[which][1])
            return carry

        lax.fori_loop(0, pairs, attend, 0)

    for target in range(n - 1, 0, -1):

        @pl.when(ctx < target)
        def _():
            z_copy(ctx, target).wait_send()

    for shard in range(n - 2, -1, -1):

        @pl.when(shard < ctx)
        def _():
            for step in range(1, n_head):
                x_copy(shard, head, step).wait_send()
            for step in range(1, n_sub):
                for x in range(n_head):
                    s_copy(shard, x, sub, step).wait_send()


def per_device(n, n_head, n_sub, queries, latent, rope_keys, latent_gain, up_weight, prompt_length):
    rows, width = latent.shape
    pairs = up_weight.shape[1] // (2 * KVDIM)
    heads = 2 * pairs
    tokens = n * rows
    chunk = tokens if tokens <= 512 else (512 if tokens % 512 == 0 else rows)
    anywhere = pl.BlockSpec(memory_space=pl.ANY)
    dma = pltpu.SemaphoreType.DMA
    cost = pl.CostEstimate(
        flops=2 * tokens * width * up_weight.shape[1] + 2 * heads * rows * tokens * (QDIM + VDIM),
        bytes_accessed=2 * (queries.size + up_weight.size + rows * heads * VDIM),
        transcendentals=heads * rows * tokens,
    )
    return pl.pallas_call(
        functools.partial(kernel, n, n_head, n_sub, chunk),
        out_shape=pltpu.VMEM((rows, heads * VDIM), jnp.bfloat16),
        in_specs=[pl.BlockSpec(memory_space=pltpu.SMEM)] + [anywhere] * 5,
        out_specs=pl.BlockSpec(memory_space=pltpu.VMEM),
        scratch_shapes=[
            pltpu.VMEM((tokens, width + 2 * ROPE), jnp.bfloat16),
            pltpu.VMEM(queries.shape, jnp.bfloat16),
            pltpu.VMEM((heads, rows, NOPE + 2 * ROPE), jnp.bfloat16),
            pltpu.VMEM((pairs, width, 2 * KVDIM), jnp.bfloat16),
            pltpu.VMEM((pairs if chunk == tokens else 1, chunk, 2 * KVDIM), jnp.bfloat16),
            pltpu.VMEM((rows, width), jnp.bfloat16),
            pltpu.VMEM((ROPE, rows), jnp.bfloat16),
            pltpu.VMEM((width,), jnp.float32),
            dma((4,)),
            dma((pairs,)),
            dma((n,)),
            dma((n,)),
            dma((n, n_head)),
            dma((n, n_head)),
            dma((n, n_head, n_sub)),
            dma((n, n_head, n_sub)),
        ],
        compiler_params=pltpu.CompilerParams(
            collective_id=0, has_side_effects=True, vmem_limit_bytes=63 * 1024 * 1024
        ),
        cost_estimate=cost,
        name="mla_prefill",
    )(prompt_length, queries, latent, rope_keys.T, latent_gain, up_weight)


def solution(mesh):
    placed = (
        P(("parts", "ctx"), ("head", "sub")),
        P(("parts", "ctx"), None),
        P(("parts", "ctx"), None),
        P(),
        P(None, ("head", "sub")),
        P("parts"),
    )
    return jax.shard_map(
        functools.partial(per_device, mesh.shape["ctx"], mesh.shape["head"], mesh.shape["sub"]),
        mesh=mesh,
        in_specs=placed,
        out_specs=P(("parts", "ctx"), ("head", "sub")),
        check_vma=False,
    )
```

```python
import functools
import math

import jax
import jax.numpy as jnp
from jax import lax
from jax.experimental import pallas as pl
from jax.experimental.pallas import tpu as pltpu
from jax.sharding import PartitionSpec as P

ROPE = 64
NOPE = 128
VDIM = 128
QDIM = NOPE + ROPE
KVDIM = NOPE + VDIM
MESH = pl.DeviceIdType.MESH
SCORE_SCALE = math.log2(math.e) / math.sqrt(NOPE + ROPE)


def angle_tables(first_pos, rows):
    lane8 = lax.broadcasted_iota(jnp.int32, (8, 2 * ROPE), 1)
    half = ROPE // 2
    frequency = jnp.exp((lane8 % half).astype(jnp.float32) * (-math.log(10000.0) / half))
    low = lax.broadcasted_iota(jnp.int32, (8, 2 * ROPE), 0).astype(jnp.float32) * frequency
    blocks = rows // 8
    lane = lax.broadcasted_iota(jnp.int32, (blocks, 2 * ROPE), 1)
    block_frequency = jnp.exp((lane % half).astype(jnp.float32) * (-math.log(10000.0) / half))
    base = (first_pos + 8 * lax.broadcasted_iota(jnp.int32, (blocks, 2 * ROPE), 0)).astype(jnp.float32)
    high = base * block_frequency
    cos_low, sin_low = jnp.cos(low), jnp.sin(low)
    cos_high, sin_high = jnp.cos(high), jnp.sin(high)
    cosines, sines = [], []
    for block in range(blocks):
        ch, sh = cos_high[block : block + 1], sin_high[block : block + 1]
        cosines.append(ch * cos_low - sh * sin_low)
        sines.append(sh * cos_low + ch * sin_low)
    cosine = jnp.concatenate(cosines, 0)
    sine = jnp.concatenate(sines, 0)
    lane = lax.broadcasted_iota(jnp.int32, (rows, 2 * ROPE), 1)
    return cosine, jnp.where(lane % ROPE < half, -sine, sine)


def rotate_pair(values, cosine, sine):
    half = ROPE // 2
    lane = lax.broadcasted_iota(jnp.int32, values.shape, 1)
    swapped = jnp.where(
        lane % ROPE < half, pltpu.roll(values, 2 * ROPE - half, 1), pltpu.roll(values, half, 1)
    )
    return values * cosine + swapped * sine


def kernel(
    n, n_head, n_sub, chunk,
    length_ref, queries, latent, rope_keys, latent_gain, up_weight, out,
    keys, q_raw, q_ready, w_buf, kv, lat_buf, rope_buf, gain_buf,
    load_sem, w_sem, z_send, z_recv, x_send, x_recv, s_send, s_recv,
):
    ctx = lax.axis_index("ctx")
    head = lax.axis_index("head")
    sub = lax.axis_index("sub")
    rows = latent.shape[0]
    width = latent.shape[1]
    pairs = w_buf.shape[0]
    pair_w = 2 * KVDIM
    pair_q = 2 * QDIM
    piece = rows // (n_head * n_sub)
    others = (n - 1) * rows
    n_chunks = n * rows // chunk

    loads = [
        pltpu.make_async_copy(latent, lat_buf, load_sem.at[0]),
        pltpu.make_async_copy(rope_keys, rope_buf, load_sem.at[1]),
        pltpu.make_async_copy(latent_gain, gain_buf, load_sem.at[2]),
        pltpu.make_async_copy(queries, q_raw, load_sem.at[3]),
    ]
    for load in loads:
        load.start()

    def w_load(pair):
        return pltpu.make_async_copy(
            up_weight.at[:, pl.ds(pl.multiple_of(pair * pair_w, pair_w), pair_w)],
            w_buf.at[pair],
            w_sem.at[pair],
        )

    for pair in range(pairs):
        w_load(pair).start()

    barrier = pltpu.get_barrier_semaphore()
    for other in range(n - 1):

        @pl.when(other < ctx)
        def _():
            pl.semaphore_signal(barrier, inc=1, device_id={"ctx": other}, device_id_type=MESH)

    @pl.when(ctx > 0)
    def _():
        for step in range(1, n_head):
            pl.semaphore_signal(
                barrier, inc=1, device_id={"head": lax.rem(head + step, n_head)}, device_id_type=MESH
            )
        for step in range(1, n_sub):
            pl.semaphore_signal(
                barrier, inc=1, device_id={"sub": lax.rem(sub + step, n_sub)}, device_id_type=MESH
            )
            for h_step in range(1, n_head):
                pl.semaphore_signal(
                    barrier, inc=1,
                    device_id={"head": lax.rem(head + h_step, n_head), "sub": lax.rem(sub + step, n_sub)},
                    device_id_type=MESH,
                )

    cosine, sine = angle_tables(ctx * rows, rows)

    loads[0].wait()
    loads[1].wait()
    loads[2].wait()
    widened = lat_buf[...].astype(jnp.float32)
    mean = jnp.mean(widened * widened, -1, keepdims=True)
    normed = (widened * lax.rsqrt(mean + 1e-06) * gain_buf[...].reshape(1, width)).astype(jnp.bfloat16)
    rope = rope_buf[...].astype(jnp.float32)
    rope = jnp.concatenate([rope, rope], 0).T
    rotated = rotate_pair(rope, cosine, sine).astype(jnp.bfloat16)
    own = pl.ds(others, rows)
    keys[own, pl.ds(0, width)] = normed
    keys[own, pl.ds(width, 2 * ROPE)] = rotated

    for slot in range(n - 1):

        @pl.when(ctx <= slot)
        def _():
            keys[pl.ds(slot * rows, rows), :] = jnp.zeros((rows, width + 2 * ROPE), jnp.bfloat16)

    loads[3].wait()
    lane = lax.broadcasted_iota(jnp.int32, (rows, 2 * ROPE), 1)
    lower = lane < ROPE

    def ready(pair, carry):
        at = pl.multiple_of(pair * pair_q, 128)
        tile1 = q_raw[:, pl.ds(at + NOPE, 128)].astype(jnp.float32)
        tile2 = q_raw[:, pl.ds(at + 2 * NOPE, 128)].astype(jnp.float32)
        spun = rotate_pair(jnp.where(lower, tile1, tile2), cosine, sine)
        q_ready[2 * pair, :, :NOPE] = q_raw[:, pl.ds(at, NOPE)]
        q_ready[2 * pair, :, NOPE:] = jnp.where(lower, spun, 0.0).astype(jnp.bfloat16)
        q_ready[2 * pair + 1, :, :NOPE] = pltpu.roll(
            jnp.where(lower, tile2, tile1), ROPE, 1
        ).astype(jnp.bfloat16)
        q_ready[2 * pair + 1, :, NOPE:] = jnp.where(lower, 0.0, spun).astype(jnp.bfloat16)
        return carry

    lax.fori_loop(0, pairs, ready, 0)

    waits = jnp.where(ctx > 0, n_head * n_sub - 1, 0) + (n - 1 - ctx)
    pl.semaphore_wait(barrier, waits)

    def rows_of(slot, x, s):
        return pl.ds(pl.multiple_of(slot * rows + (x * n_sub + s) * piece, piece), piece)

    def z_copy(shard, target):
        return pltpu.make_async_remote_copy(
            keys.at[rows_of(n - 1, head, sub)], keys.at[rows_of(shard, head, sub)],
            z_send.at[target], z_recv.at[shard],
            device_id={"ctx": target}, device_id_type=MESH,
        )

    def x_copy(shard, x, step):
        where = keys.at[rows_of(shard, x, sub)]
        return pltpu.make_async_remote_copy(
            where, where, x_send.at[shard, step], x_recv.at[shard, x],
            device_id={"head": lax.rem(head + step, n_head)}, device_id_type=MESH,
        )

    def s_copy(shard, x, s, step):
        where = keys.at[rows_of(shard, x, s)]
        return pltpu.make_async_remote_copy(
            where, where, s_send.at[shard, x, step], s_recv.at[shard, x, s],
            device_id={"sub": lax.rem(sub + step, n_sub)}, device_id_type=MESH,
        )

    def diagonal_copy(shard, h_step, step):
        where = keys.at[rows_of(shard, head, sub)]
        to_head = lax.rem(head + h_step, n_head)
        return pltpu.make_async_remote_copy(
            where, where, s_send.at[shard, to_head, step], s_recv.at[shard, head, sub],
            device_id={"head": to_head, "sub": lax.rem(sub + step, n_sub)}, device_id_type=MESH,
        )

    for target in range(n - 1, 0, -1):

        @pl.when(ctx < target)
        def _():
            z_copy(ctx, target).start()

    def project(block, pair):
        return jnp.dot(
            keys[block, pl.ds(0, width)], w_buf[pair], preferred_element_type=jnp.float32
        ).astype(jnp.bfloat16)

    def expand(block, first, last, fresh):
        def one(pair, carry):
            if fresh:
                w_load(pair).wait()
            kv[pair, block, :] = project(block, pair)
            return carry

        lax.fori_loop(first, last, one, 0, unroll=2)

    def pass_on(shard):
        @pl.when(shard < ctx)
        def _():
            z_copy(shard, ctx).wait_recv()
            for step in range(1, n_head):
                x_copy(shard, head, step).start()
            for step in range(1, n_sub):
                s_copy(shard, head, sub, step).start()
                if shard == 0:
                    for h_step in range(1, n_head):
                        diagonal_copy(shard, h_step, step).start()

    def pass_to_sibling(shard):
        @pl.when(shard < ctx)
        def _():
            for step in range(1, n_head):
                x = lax.rem(head + step, n_head)
                x_copy(shard, x, step).wait_recv()
                for s_step in range(1, n_sub if shard else 1):
                    s_copy(shard, x, sub, s_step).start()

    def complete(shard):
        for x in range(n_head):
            for s_step in range(1, n_sub):
                s_copy(shard, x, lax.rem(sub + s_step, n_sub), s_step).wait_recv()

    order = list(range(n - 2, -1, -1))
    if n_chunks == 1:
        expand(own, 0, pairs // 2, True)
    else:
        for pair in range(pairs):
            w_load(pair).wait()
    for shard in order:
        pass_on(shard)
    if n_chunks == 1:
        expand(own, pairs // 2, pairs, True)
    for shard in order:
        pass_to_sibling(shard)
    for shard in order:

        @pl.when(shard < ctx)
        def _():
            complete(shard)

    length = length_ref[0]
    row_pos = ctx * rows + lax.broadcasted_iota(jnp.int32, (rows, 1), 0)
    last_key = jnp.minimum(row_pos, length - 1)
    live = row_pos < length

    def allowed_keys(first):
        slot_pos = first + lax.broadcasted_iota(jnp.int32, (1, chunk), 1)
        far = n * rows
        position = jnp.where(
            slot_pos >= others, slot_pos - others + ctx * rows, jnp.where(slot_pos < ctx * rows, slot_pos, far)
        )
        return position <= last_key

    def head_scores(pair, which, key_nope, key_rope, allowed):
        k = jnp.concatenate([key_nope, key_rope], 1)
        scores = lax.dot_general(
            q_ready[2 * pair + which], k, (((1,), (1,)), ((), ())), preferred_element_type=jnp.float32
        )
        return jnp.where(allowed, scores, -1e30)

    def head_mix(weights, values):
        v = jnp.concatenate([values, jnp.ones_like(values)], 1)
        return jnp.dot(weights.astype(jnp.bfloat16), v, preferred_element_type=jnp.float32)

    def finish(pair, which, mixed):
        result = jnp.where(live, mixed[:, :VDIM] / mixed[:, VDIM:], 0.0)
        at = pl.multiple_of((2 * pair + which) * VDIM, VDIM)
        out[:, pl.ds(at, VDIM)] = result.astype(jnp.bfloat16)

    if n_chunks == 1:
        allowed = allowed_keys(0)

        expand(pl.ds(0, others), 0, pairs, False)
        together = 4 if pairs % 2 == 0 else 2

        def attend(step, carry):
            where = [(step * (together // 2) + k // 2, k % 2) for k in range(together)]
            key_rope = keys[:, pl.ds(width, 2 * ROPE)]
            scores = [
                head_scores(
                    pair, which, kv[pair, :, which * KVDIM : which * KVDIM + NOPE], key_rope, allowed
                )
                for pair, which in where
            ]
            tops = [jnp.max(score, -1, keepdims=True) for score in scores]
            weights = [
                jnp.exp2((score - top) * SCORE_SCALE).astype(jnp.bfloat16)
                for score, top in zip(scores, tops)
            ]
            mixes = [
                head_mix(weight, kv[pair, :, which * KVDIM + NOPE : (which + 1) * KVDIM])
                for (pair, which), weight in zip(where, weights)
            ]
            for (pair, which), mixed in zip(where, mixes):
                finish(pair, which, mixed)
            return carry

        lax.fori_loop(0, 2 * pairs // together, attend, 0)
    else:

        def attend(pair, carry):
            needed = jnp.minimum((ctx * rows + chunk - 1) // chunk, n_chunks - 1)

            def one_chunk(step, state):
                index = jnp.where(step == needed, n_chunks - 1, step)
                at = pl.multiple_of(index * chunk, chunk)
                block = pl.ds(at, chunk)
                expanded = project(block, pair)
                allowed = allowed_keys(at)
                later = []
                for which in range(2):
                    top, mixed = state[which]
                    first = which * KVDIM
                    scores = head_scores(
                        pair, which, expanded[:, first : first + NOPE],
                        keys[block, pl.ds(width, 2 * ROPE)], allowed,
                    )
                    new_top = jnp.maximum(top, jnp.max(scores, -1, keepdims=True))
                    weights = jnp.where(allowed, jnp.exp2((scores - new_top) * SCORE_SCALE), 0.0)
                    fade = jnp.exp2((top - new_top) * SCORE_SCALE)
                    mix = head_mix(weights, expanded[:, first + NOPE : first + KVDIM])
                    later.append((new_top, mixed * fade + mix))
                return tuple(later)

            blank = (jnp.full((rows, 1), -1e30, jnp.float32), jnp.zeros((rows, 2 * VDIM), jnp.float32))
            state = lax.fori_loop(0, needed + 1, one_chunk, (blank, blank))
            for which in range(2):
                finish(pair, which, state[which][1])
            return carry

        lax.fori_loop(0, pairs, attend, 0)

    for target in range(n - 1, 0, -1):

        @pl.when(ctx < target)
        def _():
            z_copy(ctx, target).wait_send()

    for shard in range(n - 2, -1, -1):

        @pl.when(shard < ctx)
        def _():
            for step in range(1, n_head):
                x_copy(shard, head, step).wait_send()
            for step in range(1, n_sub):
                for x in range(n_head):
                    s_copy(shard, x, sub, step).wait_send()


def per_device(n, n_head, n_sub, queries, latent, rope_keys, latent_gain, up_weight, prompt_length):
    rows, width = latent.shape
    pairs = up_weight.shape[1] // (2 * KVDIM)
    heads = 2 * pairs
    tokens = n * rows
    chunk = tokens if tokens <= 512 else (512 if tokens % 512 == 0 else rows)
    anywhere = pl.BlockSpec(memory_space=pl.ANY)
    dma = pltpu.SemaphoreType.DMA
    cost = pl.CostEstimate(
        flops=2 * tokens * width * up_weight.shape[1] + 2 * heads * rows * tokens * (QDIM + VDIM),
        bytes_accessed=2 * (queries.size + up_weight.size + rows * heads * VDIM),
        transcendentals=heads * rows * tokens,
    )
    return pl.pallas_call(
        functools.partial(kernel, n, n_head, n_sub, chunk),
        out_shape=pltpu.VMEM((rows, heads * VDIM), jnp.bfloat16),
        in_specs=[pl.BlockSpec(memory_space=pltpu.SMEM)] + [anywhere] * 5,
        out_specs=pl.BlockSpec(memory_space=pltpu.VMEM),
        scratch_shapes=[
            pltpu.VMEM((tokens, width + 2 * ROPE), jnp.bfloat16),
            pltpu.VMEM(queries.shape, jnp.bfloat16),
            pltpu.VMEM((heads, rows, NOPE + 2 * ROPE), jnp.bfloat16),
            pltpu.VMEM((pairs, width, 2 * KVDIM), jnp.bfloat16),
            pltpu.VMEM((pairs if chunk == tokens else 1, chunk, 2 * KVDIM), jnp.bfloat16),
            pltpu.VMEM((rows, width), jnp.bfloat16),
            pltpu.VMEM((ROPE, rows), jnp.bfloat16),
            pltpu.VMEM((width,), jnp.float32),
            dma((4,)),
            dma((pairs,)),
            dma((n,)),
            dma((n,)),
            dma((n, n_head)),
            dma((n, n_head)),
            dma((n, n_head, n_sub)),
            dma((n, n_head, n_sub)),
        ],
        compiler_params=pltpu.CompilerParams(
            collective_id=0, has_side_effects=True, vmem_limit_bytes=63 * 1024 * 1024
        ),
        cost_estimate=cost,
        name="mla_prefill",
    )(prompt_length, queries, latent, rope_keys.T, latent_gain, up_weight)


def solution(mesh):
    placed = (
        P(("parts", "ctx"), ("head", "sub")),
        P(("parts", "ctx"), None),
        P(("parts", "ctx"), None),
        P(),
        P(None, ("head", "sub")),
        P("parts"),
    )
    return jax.shard_map(
        functools.partial(per_device, mesh.shape["ctx"], mesh.shape["head"], mesh.shape["sub"]),
        mesh=mesh,
        in_specs=placed,
        out_specs=P(("parts", "ctx"), ("head", "sub")),
        check_vma=False,
    )
```

```python
import functools
import math

import jax
import jax.numpy as jnp
from jax import lax
from jax.experimental import pallas as pl
from jax.experimental.pallas import tpu as pltpu
from jax.sharding import PartitionSpec as P

ROPE = 64
NOPE = 128
VDIM = 128
QDIM = NOPE + ROPE
KVDIM = NOPE + VDIM
MESH = pl.DeviceIdType.MESH
SCORE_SCALE = math.log2(math.e) / math.sqrt(NOPE + ROPE)


def angle_tables(first_pos, rows):
    lane8 = lax.broadcasted_iota(jnp.int32, (8, 2 * ROPE), 1)
    half = ROPE // 2
    frequency = jnp.exp((lane8 % half).astype(jnp.float32) * (-math.log(10000.0) / half))
    low = lax.broadcasted_iota(jnp.int32, (8, 2 * ROPE), 0).astype(jnp.float32) * frequency
    blocks = rows // 8
    lane = lax.broadcasted_iota(jnp.int32, (blocks, 2 * ROPE), 1)
    block_frequency = jnp.exp((lane % half).astype(jnp.float32) * (-math.log(10000.0) / half))
    base = (first_pos + 8 * lax.broadcasted_iota(jnp.int32, (blocks, 2 * ROPE), 0)).astype(jnp.float32)
    high = base * block_frequency
    cos_low, sin_low = jnp.cos(low), jnp.sin(low)
    cos_high, sin_high = jnp.cos(high), jnp.sin(high)
    cosines, sines = [], []
    for block in range(blocks):
        ch, sh = cos_high[block : block + 1], sin_high[block : block + 1]
        cosines.append(ch * cos_low - sh * sin_low)
        sines.append(sh * cos_low + ch * sin_low)
    cosine = jnp.concatenate(cosines, 0)
    sine = jnp.concatenate(sines, 0)
    lane = lax.broadcasted_iota(jnp.int32, (rows, 2 * ROPE), 1)
    return cosine, jnp.where(lane % ROPE < half, -sine, sine)


def rotate_pair(values, cosine, sine):
    half = ROPE // 2
    lane = lax.broadcasted_iota(jnp.int32, values.shape, 1)
    swapped = jnp.where(
        lane % ROPE < half, pltpu.roll(values, 2 * ROPE - half, 1), pltpu.roll(values, half, 1)
    )
    return values * cosine + swapped * sine


def kernel(
    n, n_head, n_sub, chunk,
    length_ref, queries, latent, rope_keys, latent_gain, up_weight, out,
    keys, q_raw, q_ready, w_buf, kv, lat_buf, rope_buf, gain_buf,
    load_sem, w_sem, z_send, z_recv, x_send, x_recv, s_send, s_recv,
):
    ctx = lax.axis_index("ctx")
    head = lax.axis_index("head")
    sub = lax.axis_index("sub")
    rows = latent.shape[0]
    width = latent.shape[1]
    pairs = w_buf.shape[0]
    pair_w = 2 * KVDIM
    pair_q = 2 * QDIM
    piece = rows // (n_head * n_sub)
    others = (n - 1) * rows
    n_chunks = n * rows // chunk

    loads = [
        pltpu.make_async_copy(latent, lat_buf, load_sem.at[0]),
        pltpu.make_async_copy(rope_keys, rope_buf, load_sem.at[1]),
        pltpu.make_async_copy(latent_gain, gain_buf, load_sem.at[2]),
        pltpu.make_async_copy(queries, q_raw, load_sem.at[3]),
    ]
    for load in loads:
        load.start()

    def w_load(pair):
        return pltpu.make_async_copy(
            up_weight.at[:, pl.ds(pl.multiple_of(pair * pair_w, pair_w), pair_w)],
            w_buf.at[pair],
            w_sem.at[pair],
        )

    for pair in range(pairs):
        w_load(pair).start()

    barrier = pltpu.get_barrier_semaphore()
    for other in range(n - 1):

        @pl.when(other < ctx)
        def _():
            pl.semaphore_signal(barrier, inc=1, device_id={"ctx": other}, device_id_type=MESH)

    @pl.when(ctx > 0)
    def _():
        for step in range(1, n_head):
            pl.semaphore_signal(
                barrier, inc=1, device_id={"head": lax.rem(head + step, n_head)}, device_id_type=MESH
            )
        for step in range(1, n_sub):
            pl.semaphore_signal(
                barrier, inc=1, device_id={"sub": lax.rem(sub + step, n_sub)}, device_id_type=MESH
            )

    cosine, sine = angle_tables(ctx * rows, rows)

    loads[0].wait()
    loads[1].wait()
    loads[2].wait()
    widened = lat_buf[...].astype(jnp.float32)
    mean = jnp.mean(widened * widened, -1, keepdims=True)
    normed = (widened * lax.rsqrt(mean + 1e-06) * gain_buf[...].reshape(1, width)).astype(jnp.bfloat16)
    rope = rope_buf[...].astype(jnp.float32)
    rope = jnp.concatenate([rope, rope], 0).T
    rotated = rotate_pair(rope, cosine, sine).astype(jnp.bfloat16)
    own = pl.ds(others, rows)
    keys[own, pl.ds(0, width)] = normed
    keys[own, pl.ds(width, 2 * ROPE)] = rotated

    for slot in range(n - 1):

        @pl.when(ctx <= slot)
        def _():
            keys[pl.ds(slot * rows, rows), :] = jnp.zeros((rows, width + 2 * ROPE), jnp.bfloat16)

    loads[3].wait()
    lane = lax.broadcasted_iota(jnp.int32, (rows, 2 * ROPE), 1)
    lower = lane < ROPE

    def ready(pair, carry):
        at = pl.multiple_of(pair * pair_q, 128)
        tile1 = q_raw[:, pl.ds(at + NOPE, 128)].astype(jnp.float32)
        tile2 = q_raw[:, pl.ds(at + 2 * NOPE, 128)].astype(jnp.float32)
        spun = rotate_pair(jnp.where(lower, tile1, tile2), cosine, sine)
        q_ready[2 * pair, :, :NOPE] = q_raw[:, pl.ds(at, NOPE)]
        q_ready[2 * pair, :, NOPE:] = jnp.where(lower, spun, 0.0).astype(jnp.bfloat16)
        q_ready[2 * pair + 1, :, :NOPE] = pltpu.roll(
            jnp.where(lower, tile2, tile1), ROPE, 1
        ).astype(jnp.bfloat16)
        q_ready[2 * pair + 1, :, NOPE:] = jnp.where(lower, 0.0, spun).astype(jnp.bfloat16)
        return carry

    lax.fori_loop(0, pairs, ready, 0)

    waits = jnp.where(ctx > 0, n_head - 1 + n_sub - 1, 0) + (n - 1 - ctx)
    pl.semaphore_wait(barrier, waits)

    def rows_of(slot, x, s):
        return pl.ds(pl.multiple_of(slot * rows + (x * n_sub + s) * piece, piece), piece)

    def z_copy(shard, target):
        return pltpu.make_async_remote_copy(
            keys.at[rows_of(n - 1, head, sub)], keys.at[rows_of(shard, head, sub)],
            z_send.at[target], z_recv.at[shard],
            device_id={"ctx": target}, device_id_type=MESH,
        )

    def x_copy(shard, x, step):
        where = keys.at[rows_of(shard, x, sub)]
        return pltpu.make_async_remote_copy(
            where, where, x_send.at[shard, step], x_recv.at[shard, x],
            device_id={"head": lax.rem(head + step, n_head)}, device_id_type=MESH,
        )

    def s_copy(shard, x, s, step):
        where = keys.at[rows_of(shard, x, s)]
        return pltpu.make_async_remote_copy(
            where, where, s_send.at[shard, x, step], s_recv.at[shard, x, s],
            device_id={"sub": lax.rem(sub + step, n_sub)}, device_id_type=MESH,
        )

    for target in range(n - 1, 0, -1):

        @pl.when(ctx < target)
        def _():
            z_copy(ctx, target).start()

    def project(block, pair):
        return jnp.dot(
            keys[block, pl.ds(0, width)], w_buf[pair], preferred_element_type=jnp.float32
        ).astype(jnp.bfloat16)

    def expand(block, first, last, fresh):
        def one(pair, carry):
            if fresh:
                w_load(pair).wait()
            kv[pair, block, :] = project(block, pair)
            return carry

        lax.fori_loop(first, last, one, 0, unroll=4)

    def pass_on(shard):
        @pl.when(shard < ctx)
        def _():
            z_copy(shard, ctx).wait_recv()
            for step in range(1, n_head):
                x_copy(shard, head, step).start()
            for step in range(1, n_sub):
                s_copy(shard, head, sub, step).start()

    def pass_to_sibling(shard):
        @pl.when(shard < ctx)
        def _():
            for step in range(1, n_head):
                x = lax.rem(head + step, n_head)
                x_copy(shard, x, step).wait_recv()
                for s_step in range(1, n_sub):
                    s_copy(shard, x, sub, s_step).start()

    def complete(shard):
        for x in range(n_head):
            for s_step in range(1, n_sub):
                s_copy(shard, x, lax.rem(sub + s_step, n_sub), s_step).wait_recv()

    order = list(range(n - 2, -1, -1))
    if n_chunks == 1:
        expand(own, 0, pairs // 2, True)
    else:
        for pair in range(pairs):
            w_load(pair).wait()
    for shard in order:
        pass_on(shard)
    if n_chunks == 1:
        expand(own, pairs // 2, pairs, True)
    for shard in order:
        pass_to_sibling(shard)
    for shard in order:

        @pl.when(shard < ctx)
        def _():
            complete(shard)

    length = length_ref[0]
    row_pos = ctx * rows + lax.broadcasted_iota(jnp.int32, (rows, 1), 0)
    last_key = jnp.minimum(row_pos, length - 1)
    live = row_pos < length

    def allowed_keys(first):
        slot_pos = first + lax.broadcasted_iota(jnp.int32, (1, chunk), 1)
        far = n * rows
        position = jnp.where(
            slot_pos >= others, slot_pos - others + ctx * rows, jnp.where(slot_pos < ctx * rows, slot_pos, far)
        )
        return position <= last_key

    def head_scores(pair, which, key_nope, key_rope, allowed):
        k = jnp.concatenate([key_nope, key_rope], 1)
        scores = lax.dot_general(
            q_ready[2 * pair + which], k, (((1,), (1,)), ((), ())), preferred_element_type=jnp.float32
        )
        return jnp.where(allowed, scores, -1e30)

    def head_mix(weights, values):
        v = jnp.concatenate([values, jnp.ones_like(values)], 1)
        return jnp.dot(weights.astype(jnp.bfloat16), v, preferred_element_type=jnp.float32)

    def finish(pair, which, mixed):
        result = jnp.where(live, mixed[:, :VDIM] / mixed[:, VDIM:], 0.0)
        at = pl.multiple_of((2 * pair + which) * VDIM, VDIM)
        out[:, pl.ds(at, VDIM)] = result.astype(jnp.bfloat16)

    if n_chunks == 1:
        allowed = allowed_keys(0)

        expand(pl.ds(0, others), 0, pairs, False)
        together = 8 if pairs % 4 == 0 else 2

        def attend(step, carry):
            where = [(step * (together // 2) + k // 2, k % 2) for k in range(together)]
            key_rope = keys[:, pl.ds(width, 2 * ROPE)]
            scores = [
                head_scores(
                    pair, which, kv[pair, :, which * KVDIM : which * KVDIM + NOPE], key_rope, allowed
                )
                for pair, which in where
            ]
            tops = [jnp.max(score, -1, keepdims=True) for score in scores]
            weights = [
                jnp.exp2((score - top) * SCORE_SCALE).astype(jnp.bfloat16)
                for score, top in zip(scores, tops)
            ]
            mixes = [
                head_mix(weight, kv[pair, :, which * KVDIM + NOPE : (which + 1) * KVDIM])
                for (pair, which), weight in zip(where, weights)
            ]
            for (pair, which), mixed in zip(where, mixes):
                finish(pair, which, mixed)
            return carry

        lax.fori_loop(0, 2 * pairs // together, attend, 0)
    else:

        def attend(pair, carry):
            needed = jnp.minimum((ctx * rows + chunk - 1) // chunk, n_chunks - 1)

            def one_chunk(step, state):
                index = jnp.where(step == needed, n_chunks - 1, step)
                at = pl.multiple_of(index * chunk, chunk)
                block = pl.ds(at, chunk)
                expanded = project(block, pair)
                allowed = allowed_keys(at)
                later = []
                for which in range(2):
                    top, mixed = state[which]
                    first = which * KVDIM
                    scores = head_scores(
                        pair, which, expanded[:, first : first + NOPE],
                        keys[block, pl.ds(width, 2 * ROPE)], allowed,
                    )
                    new_top = jnp.maximum(top, jnp.max(scores, -1, keepdims=True))
                    weights = jnp.where(allowed, jnp.exp2((scores - new_top) * SCORE_SCALE), 0.0)
                    fade = jnp.exp2((top - new_top) * SCORE_SCALE)
                    mix = head_mix(weights, expanded[:, first + NOPE : first + KVDIM])
                    later.append((new_top, mixed * fade + mix))
                return tuple(later)

            blank = (jnp.full((rows, 1), -1e30, jnp.float32), jnp.zeros((rows, 2 * VDIM), jnp.float32))
            state = lax.fori_loop(0, needed + 1, one_chunk, (blank, blank))
            for which in range(2):
                finish(pair, which, state[which][1])
            return carry

        lax.fori_loop(0, pairs, attend, 0)

    for target in range(n - 1, 0, -1):

        @pl.when(ctx < target)
        def _():
            z_copy(ctx, target).wait_send()

    for shard in range(n - 2, -1, -1):

        @pl.when(shard < ctx)
        def _():
            for step in range(1, n_head):
                x_copy(shard, head, step).wait_send()
            for step in range(1, n_sub):
                for x in range(n_head):
                    s_copy(shard, x, sub, step).wait_send()


def per_device(n, n_head, n_sub, queries, latent, rope_keys, latent_gain, up_weight, prompt_length):
    rows, width = latent.shape
    pairs = up_weight.shape[1] // (2 * KVDIM)
    heads = 2 * pairs
    tokens = n * rows
    chunk = tokens if tokens <= 512 else (512 if tokens % 512 == 0 else rows)
    anywhere = pl.BlockSpec(memory_space=pl.ANY)
    dma = pltpu.SemaphoreType.DMA
    cost = pl.CostEstimate(
        flops=2 * tokens * width * up_weight.shape[1] + 2 * heads * rows * tokens * (QDIM + VDIM),
        bytes_accessed=2 * (queries.size + up_weight.size + rows * heads * VDIM),
        transcendentals=heads * rows * tokens,
    )
    return pl.pallas_call(
        functools.partial(kernel, n, n_head, n_sub, chunk),
        out_shape=pltpu.VMEM((rows, heads * VDIM), jnp.bfloat16),
        in_specs=[pl.BlockSpec(memory_space=pltpu.SMEM)] + [anywhere] * 5,
        out_specs=pl.BlockSpec(memory_space=pltpu.VMEM),
        scratch_shapes=[
            pltpu.VMEM((tokens, width + 2 * ROPE), jnp.bfloat16),
            pltpu.VMEM(queries.shape, jnp.bfloat16),
            pltpu.VMEM((heads, rows, NOPE + 2 * ROPE), jnp.bfloat16),
            pltpu.VMEM((pairs, width, 2 * KVDIM), jnp.bfloat16),
            pltpu.VMEM((pairs if chunk == tokens else 1, chunk, 2 * KVDIM), jnp.bfloat16),
            pltpu.VMEM((rows, width), jnp.bfloat16),
            pltpu.VMEM((ROPE, rows), jnp.bfloat16),
            pltpu.VMEM((width,), jnp.float32),
            dma((4,)),
            dma((pairs,)),
            dma((n,)),
            dma((n,)),
            dma((n, n_head)),
            dma((n, n_head)),
            dma((n, n_head, n_sub)),
            dma((n, n_head, n_sub)),
        ],
        compiler_params=pltpu.CompilerParams(
            collective_id=0, has_side_effects=True, vmem_limit_bytes=63 * 1024 * 1024
        ),
        cost_estimate=cost,
        name="mla_prefill",
    )(prompt_length, queries, latent, rope_keys.T, latent_gain, up_weight)


def solution(mesh):
    placed = (
        P(("parts", "ctx"), ("head", "sub")),
        P(("parts", "ctx"), None),
        P(("parts", "ctx"), None),
        P(),
        P(None, ("head", "sub")),
        P("parts"),
    )
    return jax.shard_map(
        functools.partial(per_device, mesh.shape["ctx"], mesh.shape["head"], mesh.shape["sub"]),
        mesh=mesh,
        in_specs=placed,
        out_specs=P(("parts", "ctx"), ("head", "sub")),
        check_vma=False,
    )
```

```python
import functools
import math

import jax
import jax.numpy as jnp
from jax import lax
from jax.experimental import pallas as pl
from jax.experimental.pallas import tpu as pltpu
from jax.sharding import PartitionSpec as P

ROPE = 64
NOPE = 128
VDIM = 128
QDIM = NOPE + ROPE
KVDIM = NOPE + VDIM
MESH = pl.DeviceIdType.MESH
SCORE_SCALE = math.log2(math.e) / math.sqrt(NOPE + ROPE)


def angle_tables(first_pos, rows):
    lane8 = lax.broadcasted_iota(jnp.int32, (8, 2 * ROPE), 1)
    half = ROPE // 2
    frequency = jnp.exp((lane8 % half).astype(jnp.float32) * (-math.log(10000.0) / half))
    low = lax.broadcasted_iota(jnp.int32, (8, 2 * ROPE), 0).astype(jnp.float32) * frequency
    blocks = rows // 8
    lane = lax.broadcasted_iota(jnp.int32, (blocks, 2 * ROPE), 1)
    block_frequency = jnp.exp((lane % half).astype(jnp.float32) * (-math.log(10000.0) / half))
    base = (first_pos + 8 * lax.broadcasted_iota(jnp.int32, (blocks, 2 * ROPE), 0)).astype(jnp.float32)
    high = base * block_frequency
    cos_low, sin_low = jnp.cos(low), jnp.sin(low)
    cos_high, sin_high = jnp.cos(high), jnp.sin(high)
    cosines, sines = [], []
    for block in range(blocks):
        ch, sh = cos_high[block : block + 1], sin_high[block : block + 1]
        cosines.append(ch * cos_low - sh * sin_low)
        sines.append(sh * cos_low + ch * sin_low)
    cosine = jnp.concatenate(cosines, 0)
    sine = jnp.concatenate(sines, 0)
    lane = lax.broadcasted_iota(jnp.int32, (rows, 2 * ROPE), 1)
    return cosine, jnp.where(lane % ROPE < half, -sine, sine)


def rotate_pair(values, cosine, sine):
    half = ROPE // 2
    lane = lax.broadcasted_iota(jnp.int32, values.shape, 1)
    swapped = jnp.where(
        lane % ROPE < half, pltpu.roll(values, 2 * ROPE - half, 1), pltpu.roll(values, half, 1)
    )
    return values * cosine + swapped * sine


def kernel(
    n, n_head, n_sub, chunk,
    length_ref, queries, latent, rope_keys, latent_gain, up_weight, out,
    keys, q_raw, q_ready, w_buf, kv, lat_buf, rope_buf, gain_buf,
    load_sem, w_sem, z_send, z_recv, x_send, x_recv, s_send, s_recv,
):
    ctx = lax.axis_index("ctx")
    head = lax.axis_index("head")
    sub = lax.axis_index("sub")
    rows = latent.shape[0]
    width = latent.shape[1]
    pairs = w_buf.shape[0]
    pair_w = 2 * KVDIM
    pair_q = 2 * QDIM
    piece = rows // (n_head * n_sub)
    others = (n - 1) * rows
    n_chunks = n * rows // chunk

    loads = [
        pltpu.make_async_copy(latent, lat_buf, load_sem.at[0]),
        pltpu.make_async_copy(rope_keys, rope_buf, load_sem.at[1]),
        pltpu.make_async_copy(latent_gain, gain_buf, load_sem.at[2]),
        pltpu.make_async_copy(queries, q_raw, load_sem.at[3]),
    ]
    for load in loads:
        load.start()

    def w_load(pair):
        return pltpu.make_async_copy(
            up_weight.at[:, pl.ds(pl.multiple_of(pair * pair_w, pair_w), pair_w)],
            w_buf.at[pair],
            w_sem.at[pair],
        )

    for pair in range(pairs):
        w_load(pair).start()

    barrier = pltpu.get_barrier_semaphore()
    for other in range(n - 1):

        @pl.when(other < ctx)
        def _():
            pl.semaphore_signal(barrier, inc=1, device_id={"ctx": other}, device_id_type=MESH)

    @pl.when(ctx > 0)
    def _():
        for step in range(1, n_head):
            pl.semaphore_signal(
                barrier, inc=1, device_id={"head": lax.rem(head + step, n_head)}, device_id_type=MESH
            )
        for step in range(1, n_sub):
            pl.semaphore_signal(
                barrier, inc=1, device_id={"sub": lax.rem(sub + step, n_sub)}, device_id_type=MESH
            )

    cosine, sine = angle_tables(ctx * rows, rows)

    loads[0].wait()
    loads[1].wait()
    loads[2].wait()
    widened = lat_buf[...].astype(jnp.float32)
    mean = jnp.mean(widened * widened, -1, keepdims=True)
    normed = (widened * lax.rsqrt(mean + 1e-06) * gain_buf[...].reshape(1, width)).astype(jnp.bfloat16)
    rope = rope_buf[...].astype(jnp.float32)
    rope = jnp.concatenate([rope, rope], 0).T
    rotated = rotate_pair(rope, cosine, sine).astype(jnp.bfloat16)
    own = pl.ds(others, rows)
    keys[own, pl.ds(0, width)] = normed
    keys[own, pl.ds(width, 2 * ROPE)] = rotated

    waits = jnp.where(ctx > 0, n_head - 1 + n_sub - 1, 0) + (n - 1 - ctx)
    pl.semaphore_wait(barrier, waits)

    def rows_of(slot, x, s):
        return pl.ds(pl.multiple_of(slot * rows + (x * n_sub + s) * piece, piece), piece)

    def z_copy(shard, target):
        return pltpu.make_async_remote_copy(
            keys.at[rows_of(n - 1, head, sub)], keys.at[rows_of(shard, head, sub)],
            z_send.at[target], z_recv.at[shard],
            device_id={"ctx": target}, device_id_type=MESH,
        )

    def x_copy(shard, x, step):
        where = keys.at[rows_of(shard, x, sub)]
        return pltpu.make_async_remote_copy(
            where, where, x_send.at[shard, step], x_recv.at[shard, x],
            device_id={"head": lax.rem(head + step, n_head)}, device_id_type=MESH,
        )

    def s_copy(shard, x, s, step):
        where = keys.at[rows_of(shard, x, s)]
        return pltpu.make_async_remote_copy(
            where, where, s_send.at[shard, x, step], s_recv.at[shard, x, s],
            device_id={"sub": lax.rem(sub + step, n_sub)}, device_id_type=MESH,
        )

    for target in range(n - 1, 0, -1):

        @pl.when(ctx < target)
        def _():
            z_copy(ctx, target).start()

    for slot in range(n - 1):

        @pl.when(ctx <= slot)
        def _():
            keys[pl.ds(slot * rows, rows), :] = jnp.zeros((rows, width + 2 * ROPE), jnp.bfloat16)

    loads[3].wait()
    lane = lax.broadcasted_iota(jnp.int32, (rows, 2 * ROPE), 1)
    lower = lane < ROPE

    def ready(pair, carry):
        at = pl.multiple_of(pair * pair_q, 128)
        tile1 = q_raw[:, pl.ds(at + NOPE, 128)].astype(jnp.float32)
        tile2 = q_raw[:, pl.ds(at + 2 * NOPE, 128)].astype(jnp.float32)
        spun = rotate_pair(jnp.where(lower, tile1, tile2), cosine, sine)
        q_ready[2 * pair, :, :NOPE] = q_raw[:, pl.ds(at, NOPE)]
        q_ready[2 * pair, :, NOPE:] = jnp.where(lower, spun, 0.0).astype(jnp.bfloat16)
        q_ready[2 * pair + 1, :, :NOPE] = pltpu.roll(
            jnp.where(lower, tile2, tile1), ROPE, 1
        ).astype(jnp.bfloat16)
        q_ready[2 * pair + 1, :, NOPE:] = jnp.where(lower, 0.0, spun).astype(jnp.bfloat16)
        return carry

    lax.fori_loop(0, pairs, ready, 0)

    def project(block, pair):
        return jnp.dot(
            keys[block, pl.ds(0, width)], w_buf[pair], preferred_element_type=jnp.float32
        ).astype(jnp.bfloat16)

    def expand(block, first, last, fresh):
        def one(pair, carry):
            if fresh:
                w_load(pair).wait()
            kv[pair, block, :] = project(block, pair)
            return carry

        lax.fori_loop(first, last, one, 0, unroll=4)

    def pass_on(shard):
        @pl.when(shard < ctx)
        def _():
            z_copy(shard, ctx).wait_recv()
            for step in range(1, n_head):
                x_copy(shard, head, step).start()
            for step in range(1, n_sub):
                s_copy(shard, head, sub, step).start()

    def pass_to_sibling(shard):
        @pl.when(shard < ctx)
        def _():
            for step in range(1, n_head):
                x = lax.rem(head + step, n_head)
                x_copy(shard, x, step).wait_recv()
                for s_step in range(1, n_sub):
                    s_copy(shard, x, sub, s_step).start()

    def complete(shard):
        for x in range(n_head):
            for s_step in range(1, n_sub):
                s_copy(shard, x, lax.rem(sub + s_step, n_sub), s_step).wait_recv()

    order = list(range(n - 2, -1, -1))
    if n_chunks == 1:
        expand(own, 0, pairs // 2, True)
    else:
        for pair in range(pairs):
            w_load(pair).wait()
    for shard in order:
        pass_on(shard)
    if n_chunks == 1:
        expand(own, pairs // 2, pairs, True)
    for shard in order:
        pass_to_sibling(shard)
    for shard in order:

        @pl.when(shard < ctx)
        def _():
            complete(shard)

    length = length_ref[0]
    row_pos = ctx * rows + lax.broadcasted_iota(jnp.int32, (rows, 1), 0)
    last_key = jnp.minimum(row_pos, length - 1)
    live = row_pos < length

    def allowed_keys(first):
        slot_pos = first + lax.broadcasted_iota(jnp.int32, (1, chunk), 1)
        far = n * rows
        position = jnp.where(
            slot_pos >= others, slot_pos - others + ctx * rows, jnp.where(slot_pos < ctx * rows, slot_pos, far)
        )
        return position <= last_key

    def head_scores(pair, which, key_nope, key_rope, allowed):
        k = jnp.concatenate([key_nope, key_rope], 1)
        scores = lax.dot_general(
            q_ready[2 * pair + which], k, (((1,), (1,)), ((), ())), preferred_element_type=jnp.float32
        )
        return jnp.where(allowed, scores, -1e30)

    def head_mix(weights, values):
        v = jnp.concatenate([values, jnp.ones_like(values)], 1)
        return jnp.dot(weights.astype(jnp.bfloat16), v, preferred_element_type=jnp.float32)

    def finish(pair, which, mixed):
        result = jnp.where(live, mixed[:, :VDIM] / mixed[:, VDIM:], 0.0)
        at = pl.multiple_of((2 * pair + which) * VDIM, VDIM)
        out[:, pl.ds(at, VDIM)] = result.astype(jnp.bfloat16)

    if n_chunks == 1:
        allowed = allowed_keys(0)

        expand(pl.ds(0, others), 0, pairs, False)
        together = 8 if pairs % 4 == 0 else 2

        def attend(step, carry):
            where = [(step * (together // 2) + k // 2, k % 2) for k in range(together)]
            key_rope = keys[:, pl.ds(width, 2 * ROPE)]
            scores = [
                head_scores(
                    pair, which, kv[pair, :, which * KVDIM : which * KVDIM + NOPE], key_rope, allowed
                )
                for pair, which in where
            ]
            tops = [jnp.max(score, -1, keepdims=True) for score in scores]
            weights = [
                jnp.exp2((score - top) * SCORE_SCALE).astype(jnp.bfloat16)
                for score, top in zip(scores, tops)
            ]
            mixes = [
                head_mix(weight, kv[pair, :, which * KVDIM + NOPE : (which + 1) * KVDIM])
                for (pair, which), weight in zip(where, weights)
            ]
            for (pair, which), mixed in zip(where, mixes):
                finish(pair, which, mixed)
            return carry

        lax.fori_loop(0, 2 * pairs // together, attend, 0)
    else:

        def attend(pair, carry):
            needed = jnp.minimum((ctx * rows + chunk - 1) // chunk, n_chunks - 1)

            def one_chunk(step, state):
                index = jnp.where(step == needed, n_chunks - 1, step)
                at = pl.multiple_of(index * chunk, chunk)
                block = pl.ds(at, chunk)
                expanded = project(block, pair)
                allowed = allowed_keys(at)
                later = []
                for which in range(2):
                    top, mixed = state[which]
                    first = which * KVDIM
                    scores = head_scores(
                        pair, which, expanded[:, first : first + NOPE],
                        keys[block, pl.ds(width, 2 * ROPE)], allowed,
                    )
                    new_top = jnp.maximum(top, jnp.max(scores, -1, keepdims=True))
                    weights = jnp.where(allowed, jnp.exp2((scores - new_top) * SCORE_SCALE), 0.0)
                    fade = jnp.exp2((top - new_top) * SCORE_SCALE)
                    mix = head_mix(weights, expanded[:, first + NOPE : first + KVDIM])
                    later.append((new_top, mixed * fade + mix))
                return tuple(later)

            blank = (jnp.full((rows, 1), -1e30, jnp.float32), jnp.zeros((rows, 2 * VDIM), jnp.float32))
            state = lax.fori_loop(0, needed + 1, one_chunk, (blank, blank))
            for which in range(2):
                finish(pair, which, state[which][1])
            return carry

        lax.fori_loop(0, pairs, attend, 0)

    for target in range(n - 1, 0, -1):

        @pl.when(ctx < target)
        def _():
            z_copy(ctx, target).wait_send()

    for shard in range(n - 2, -1, -1):

        @pl.when(shard < ctx)
        def _():
            for step in range(1, n_head):
                x_copy(shard, head, step).wait_send()
            for step in range(1, n_sub):
                for x in range(n_head):
                    s_copy(shard, x, sub, step).wait_send()


def per_device(n, n_head, n_sub, queries, latent, rope_keys, latent_gain, up_weight, prompt_length):
    rows, width = latent.shape
    pairs = up_weight.shape[1] // (2 * KVDIM)
    heads = 2 * pairs
    tokens = n * rows
    chunk = tokens if tokens <= 512 else (512 if tokens % 512 == 0 else rows)
    anywhere = pl.BlockSpec(memory_space=pl.ANY)
    dma = pltpu.SemaphoreType.DMA
    cost = pl.CostEstimate(
        flops=2 * tokens * width * up_weight.shape[1] + 2 * heads * rows * tokens * (QDIM + VDIM),
        bytes_accessed=2 * (queries.size + up_weight.size + rows * heads * VDIM),
        transcendentals=heads * rows * tokens,
    )
    return pl.pallas_call(
        functools.partial(kernel, n, n_head, n_sub, chunk),
        out_shape=pltpu.VMEM((rows, heads * VDIM), jnp.bfloat16),
        in_specs=[pl.BlockSpec(memory_space=pltpu.SMEM)] + [anywhere] * 5,
        out_specs=pl.BlockSpec(memory_space=pltpu.VMEM),
        scratch_shapes=[
            pltpu.VMEM((tokens, width + 2 * ROPE), jnp.bfloat16),
            pltpu.VMEM(queries.shape, jnp.bfloat16),
            pltpu.VMEM((heads, rows, NOPE + 2 * ROPE), jnp.bfloat16),
            pltpu.VMEM((pairs, width, 2 * KVDIM), jnp.bfloat16),
            pltpu.VMEM((pairs if chunk == tokens else 1, chunk, 2 * KVDIM), jnp.bfloat16),
            pltpu.VMEM((rows, width), jnp.bfloat16),
            pltpu.VMEM((ROPE, rows), jnp.bfloat16),
            pltpu.VMEM((width,), jnp.float32),
            dma((4,)),
            dma((pairs,)),
            dma((n,)),
            dma((n,)),
            dma((n, n_head)),
            dma((n, n_head)),
            dma((n, n_head, n_sub)),
            dma((n, n_head, n_sub)),
        ],
        compiler_params=pltpu.CompilerParams(
            collective_id=0, has_side_effects=True, vmem_limit_bytes=63 * 1024 * 1024
        ),
        cost_estimate=cost,
        name="mla_prefill",
    )(prompt_length, queries, latent, rope_keys.T, latent_gain, up_weight)


def solution(mesh):
    placed = (
        P(("parts", "ctx"), ("head", "sub")),
        P(("parts", "ctx"), None),
        P(("parts", "ctx"), None),
        P(),
        P(None, ("head", "sub")),
        P("parts"),
    )
    return jax.shard_map(
        functools.partial(per_device, mesh.shape["ctx"], mesh.shape["head"], mesh.shape["sub"]),
        mesh=mesh,
        in_specs=placed,
        out_specs=P(("parts", "ctx"), ("head", "sub")),
        check_vma=False,
    )
```
